256 devices in a mesh: cp: 64 (over y, z, core), tp: 4 (over x).
Axes of the slice: x: 4, y: 4, z: 8, core: 2. Of those that a mesh axis runs over, the one named last changes fastest.
Arguments:
- queries: bfloat16 [32768, 4096], P('cp', 'tp'), may hold values from -6 to 6
- key_rows: bfloat16 [32768, 512], P('cp', 'tp'), may hold values from -6 to 6
- value_rows: bfloat16 [32768, 512], P('cp', 'tp'), may hold values from -6 to 6
- out_proj: bfloat16 [4096, 4096], P('tp'), may hold values from -0.09375 to 0.09375
- grad_mixed: bfloat16 [32768, 4096], P('cp', 'tp'), may hold values from -6 to 6
- doc_start: int32 [256], replicated, may hold values from 0 to 255, as said below
- balanced_source: int32 [256], replicated, may hold values from 0 to 255, as said below
Outputs:
- mixed: bfloat16 [32768, 4096], P('cp', 'tp')
- query_grad: bfloat16 [32768, 4096], P('cp', 'tp')
- key_grad: bfloat16 [32768, 512], P('cp', 'tp')
- value_grad: bfloat16 [32768, 512], P('cp', 'tp')
The draws below stay inside these ranges and needn't reach their ends.
Inputs may be any that keep to these rules, and one draw needn't show every extreme that they name: doc_start[b] is the first block of the document that holds block b; documents are runs of 1 to 8 consecutive blocks, one of them has exactly 8, and the last block is a document of one block. `balanced_source`: a permutation of the blocks that maps each aligned run of 16 blocks onto itself.
All inputs are finite; a program needn't handle non-finite values.
Results may differ from the reference program's by a relative error of at most 0.024.
Values may be sent and summed in bfloat16 or wider, within the bound.
No kernel may reach another device: no remote copies, remote signals or barrier semaphores. Data moves between devices by JAX's collectives and lax.ppermute only.
A program may use at most 128 MiB of HBM per device.

```python
import math
import jax
import jax.numpy as jnp
from jax import lax

QH = 32
KVH = 4
HD = 128
D = 4096
BLOCK = 128
BLK_DEV = 4
MAXB = 8
GROUP = 4
NB = 256
SEQ = 32768
N_TP = 4


def draw_queries(key, part):
    key = jax.random.fold_in(key, 7)
    head_ratio = QH // KVH
    base = jnp.clip(jax.random.normal(key, (SEQ, KVH, head_ratio, HD), jnp.float32), -6.0, 6.0)
    return base.reshape(SEQ, QH * HD).astype(jnp.bfloat16)


def draw_key_rows(key, part):
    key = jax.random.fold_in(key, 11)
    base = jnp.clip(jax.random.normal(key, (SEQ, KVH, HD), jnp.float32), -6.0, 6.0)
    return base.reshape(SEQ, KVH * HD).astype(jnp.bfloat16)


def document_plan(key):
    length_key, place_key, order_key = jax.random.split(key, 3)
    blocks = jnp.arange(NB, dtype=jnp.int32)
    lengths = jax.random.randint(length_key, (NB,), 1, MAXB + 1, dtype=jnp.int32)
    chosen = jax.random.randint(place_key, (), 0, NB // MAXB - 1, dtype=jnp.int32)
    lengths = jnp.where(blocks == chosen, MAXB, lengths)
    ends = jnp.cumsum(lengths)
    doc_id = jnp.sum((ends[None, :] <= blocks[:, None]).astype(jnp.int32), axis=1)
    starts = ends - lengths
    doc_start = starts[doc_id]
    doc_start = jnp.where(blocks == NB - 1, NB - 1, doc_start)
    weight = blocks - doc_start + 1
    group_blocks = GROUP * BLK_DEV
    groups = NB // group_blocks
    ties = jax.vmap(lambda sub_key: jax.random.permutation(sub_key, group_blocks))(jax.random.split(order_key, groups))
    score = -weight.reshape(groups, group_blocks) * group_blocks + ties.astype(jnp.int32)
    ranked = jnp.argsort(score, axis=1).astype(jnp.int32)
    rank = jnp.arange(group_blocks, dtype=jnp.int32)
    round_id = rank // GROUP
    position = rank % GROUP
    member = jnp.where(round_id % 2 == 0, position, GROUP - 1 - position)
    slot = member * BLK_DEV + round_id
    local_source = jnp.zeros((groups, group_blocks), jnp.int32).at[:, slot].set(ranked)
    balanced = local_source + jnp.arange(groups, dtype=jnp.int32)[:, None] * group_blocks
    return (doc_start.astype(jnp.int32), balanced.reshape(NB).astype(jnp.int32))


def draw_doc_start(key, part):
    return document_plan(key)[0]


def draw_balanced_source(key, part):
    return document_plan(key)[1]


def shard_levels(rng, extent, cuts, smallest, top_value):
    level, own = 1.0, jax.random.fold_in(rng, 6)
    for axis_at, blocks in cuts:
        draws = jnp.exp(jax.random.uniform(jax.random.fold_in(own, axis_at), (blocks,), jnp.float32, smallest / len(cuts), top_value / len(cuts)))
        level = level * jnp.repeat(draws, extent[axis_at] // blocks).reshape([-1 if axis == axis_at else 1 for axis in range(len(extent))])
    return level


def bell_draw(own_key, extent, spread, reach, cuts=(), kind=jnp.bfloat16):
    entries = jax.random.normal(own_key, extent, jnp.float32) * spread
    if len(cuts) > 0:
        entries = shard_levels(own_key, extent, cuts, -0.22, 0.18) * entries
    return jnp.clip(entries, min=-reach, max=reach).astype(kind)


def setup_inputs(seed: int = 0) -> dict:
    keys = jax.random.split(jax.random.key(seed), 8)
    queries = draw_queries(jax.random.fold_in(keys[7], 71), 0)
    key_rows = draw_key_rows(jax.random.fold_in(keys[7], 71), 0)
    value_rows = bell_draw(keys[2], (SEQ, KVH * HD), 1.0, 6.0, ((0, 64), (1, 4)))
    out_proj = bell_draw(keys[3], (QH * HD, D), (QH * HD) ** -0.5, 0.09375, ((0, 4),))
    grad_mixed = bell_draw(keys[4], (SEQ, D), 1.0, 6.0, ((0, 64), (1, 4)))
    doc_start = draw_doc_start(jax.random.fold_in(keys[7], 71), 0)
    balanced_source = draw_balanced_source(jax.random.fold_in(keys[7], 71), 0)
    return {"queries": queries, "key_rows": key_rows, "value_rows": value_rows, "out_proj": out_proj, "grad_mixed": grad_mixed, "doc_start": doc_start, "balanced_source": balanced_source}


masked_score = -1e+30

def rounded(values):
    return lax.optimization_barrier(values.astype(jnp.bfloat16)).astype(jnp.float32)

def reference(queries, key_rows, value_rows, out_proj, grad_mixed, doc_start, balanced_source):
    head_ratio = QH // KVH
    scale_value = 1.0 / math.sqrt(HD)
    pad_blocks = MAXB - 1
    query_blocks = queries.reshape(NB, BLOCK, KVH, head_ratio, HD)
    padding = jnp.zeros((pad_blocks * BLOCK, KVH * HD), jnp.bfloat16)
    padded_keys = jnp.concatenate([padding, key_rows], 0).reshape(NB + pad_blocks, BLOCK, KVH, HD)
    padded_values = jnp.concatenate([padding, value_rows], 0).reshape(NB + pad_blocks, BLOCK, KVH, HD)
    positions = jnp.arange(BLOCK, dtype=jnp.int32)

    def allowed_pairs(block_id):
        key_block = block_id - pad_blocks + jnp.arange(MAXB, dtype=jnp.int32)
        in_document = key_block >= doc_start[block_id]
        causal_ok = (key_block[None, :, None] < block_id) | (positions[None, None, :] <= positions[:, None, None])
        return (in_document[None, :, None] & causal_ok)[None, None]

    def block_weights(block_id):
        query_block = query_blocks[block_id].astype(jnp.float32)
        key_window = lax.dynamic_slice_in_dim(padded_keys, block_id, MAXB, 0).astype(jnp.float32)
        allowed = allowed_pairs(block_id)
        scores = jnp.einsum('ikrd,mjkd->krimj', query_block, key_window) * scale_value
        scores = jnp.where(allowed, scores, masked_score)
        top_score = lax.optimization_barrier(jnp.max(scores, axis=(3, 4), keepdims=True))
        exp_total = lax.optimization_barrier(jnp.sum(jnp.exp(scores - top_score), axis=(3, 4), keepdims=True))
        log_total = top_score + jnp.log(exp_total)
        weights = rounded(jnp.where(allowed, jnp.exp(scores - log_total), 0.0))
        return (query_block, key_window, weights)

    def forward_step(running, block_id):
        query_block, key_window, weights = block_weights(block_id)
        value_window = lax.dynamic_slice_in_dim(padded_values, block_id, MAXB, 0).astype(jnp.float32)
        attended = jnp.einsum('krimj,mjkd->ikrd', weights, value_window)
        return (running, attended.astype(jnp.bfloat16).reshape(BLOCK, QH * HD))
    block_ids = jnp.arange(NB, dtype=jnp.int32)
    scan_end, attended_all = lax.scan(forward_step, jnp.zeros((), jnp.float32), block_ids)
    balanced = attended_all[balanced_source].reshape(SEQ, QH * HD)
    group_width = QH * HD // N_TP
    mixed_sum = jnp.zeros((SEQ, D), jnp.float32)
    for group_id in range(N_TP):
        head_slice = balanced[:, group_id * group_width:(group_id + 1) * group_width]
        proj_slice = out_proj[group_id * group_width:(group_id + 1) * group_width]
        mixed_sum = mixed_sum + rounded(jnp.dot(head_slice, proj_slice, preferred_element_type=jnp.float32))
    mixed = mixed_sum.astype(jnp.bfloat16)
    grad_balanced = jnp.dot(grad_mixed, out_proj.T, preferred_element_type=jnp.float32).astype(jnp.bfloat16)
    grad_packed = jnp.zeros((NB, BLOCK, QH * HD), jnp.bfloat16).at[balanced_source].set(grad_balanced.reshape(NB, BLOCK, QH * HD))
    grad_blocks = grad_packed.reshape(NB, BLOCK, KVH, head_ratio, HD)
    attended_blocks = attended_all.reshape(NB, BLOCK, KVH, head_ratio, HD)

    def backward_step(running, block_id):
        key_grad, value_grad = running
        query_block, key_window, weights = block_weights(block_id)
        value_window = lax.dynamic_slice_in_dim(padded_values, block_id, MAXB, 0).astype(jnp.float32)
        grad_block = grad_blocks[block_id].astype(jnp.float32)
        row_delta = lax.optimization_barrier(jnp.sum(grad_block * attended_blocks[block_id].astype(jnp.float32), axis=-1))
        row_delta = jnp.transpose(row_delta, (1, 2, 0))[:, :, :, None, None]
        grad_weights = jnp.einsum('ikrd,mjkd->krimj', grad_block, value_window)
        grad_scores = rounded(weights * (grad_weights - row_delta))
        query_part = jnp.einsum('krimj,mjkd->ikrd', grad_scores, key_window) * scale_value
        key_part = jnp.einsum('krimj,ikrd->mjkd', grad_scores, query_block) * scale_value
        value_part = jnp.einsum('krimj,ikrd->mjkd', weights, grad_block)
        key_grad = lax.dynamic_update_slice_in_dim(key_grad, lax.dynamic_slice_in_dim(key_grad, block_id, MAXB, 0) + key_part, block_id, 0)
        value_grad = lax.dynamic_update_slice_in_dim(value_grad, lax.dynamic_slice_in_dim(value_grad, block_id, MAXB, 0) + value_part, block_id, 0)
        return ((key_grad, value_grad), query_part.astype(jnp.bfloat16).reshape(BLOCK, QH * HD))
    zeros_grad = jnp.zeros((NB + pad_blocks, BLOCK, KVH, HD), jnp.float32)
    grad_sums, query_grad = lax.scan(backward_step, (zeros_grad, zeros_grad), block_ids)
    key_grad = grad_sums[0][pad_blocks:].reshape(SEQ, KVH * HD).astype(jnp.bfloat16)
    value_grad = grad_sums[1][pad_blocks:].reshape(SEQ, KVH * HD).astype(jnp.bfloat16)
    return (mixed, query_grad.reshape(SEQ, QH * HD), key_grad, value_grad)
```

```python
import math

import jax
import jax.numpy as jnp
from jax import lax
from jax.experimental import pallas as pl
from jax.experimental.pallas import tpu as pltpu
from jax.sharding import PartitionSpec as P

HD = 128
BLOCK = 128
BLK_DEV = 4
MAXB = 8
GROUP = 4
PRIOR = MAXB - 1
POOL = PRIOR + BLK_DEV
ROWS = BLOCK * BLK_DEV
WIDTH = 1024
CHUNKS = 2
CW = WIDTH // CHUNKS
PAIRS = CW // 256

SCALE = 1.0 / math.sqrt(HD)
SCALE_LOG2 = SCALE * math.log2(math.e)
MASKED = -1e30

START, GRAD_REL, GRAD_IDX, ATT_REL, ATT_IDX, CORE, TP = 0, 4, 8, 12, 16, 20, 21

ANY = pl.BlockSpec(memory_space=pl.ANY)
SMEM = pl.BlockSpec(memory_space=pltpu.SMEM)
VMEM_LIMIT = 48 * 1024 * 1024


def params(dims=1):
    return pltpu.CompilerParams(
        dimension_semantics=("arbitrary",) * dims, vmem_limit_bytes=VMEM_LIMIT
    )


def dot(a, b):
    return jnp.dot(a, b, preferred_element_type=jnp.float32)


def dot_nt(a, b):
    return lax.dot_general(a, b, (((1,), (1,)), ((), ())), preferred_element_type=jnp.float32)


def swap_cp(block, mask):
    count = lax.axis_size("cp")
    return lax.ppermute(block, "cp", [(i, i ^ mask) for i in range(count)])


def shift_cp(block, distance):
    count = lax.axis_size("cp")
    route = [(i, i + distance) for i in range(count) if 0 <= i + distance < count]
    return lax.ppermute(block, "cp", route)


def shift_tp(block, distance):
    count = lax.axis_size("tp")
    return lax.ppermute(block, "tp", [(i, (i + distance) % count) for i in range(count)])


def pool_copies(kv, far, near_own, near_far, keys, values, sems):
    def pair(src, row, rows, place, at):
        return [
            pltpu.make_async_copy(
                src.at[pl.ds(row, rows)], keys.at[pl.ds(place, rows)], sems.at[at]
            ),
            pltpu.make_async_copy(
                src.at[pl.ds(ROWS + row, rows)], values.at[pl.ds(place, rows)], sems.at[at + 1]
            ),
        ]

    own = pair(kv, 0, ROWS, PRIOR * BLOCK, 0)
    far_part = pair(far, BLOCK, ROWS - BLOCK, 0, 2)
    near_a = pair(near_far, 0, ROWS, ROWS - BLOCK, 4)
    near_b = pair(near_own, 0, ROWS, ROWS - BLOCK, 4)
    return own, far_part, near_a, near_b


def fill_pool(table, kv, far, near_own, near_far, keys, values, sems):
    own, far_part, near_a, near_b = pool_copies(
        kv, far, near_own, near_far, keys, values, sems
    )
    for copy in own + far_part:
        copy.start()

    @pl.when(table[CORE] == 0)
    def _():
        for copy in near_a:
            copy.start()

    @pl.when(table[CORE] != 0)
    def _():
        for copy in near_b:
            copy.start()

    for copy in own + far_part + near_a:
        copy.wait()


def transposed_pool(pool, flipped):
    for at in range(POOL):
        flipped[at] = pool[at * BLOCK : (at + 1) * BLOCK, :].T


def pair_of(flipped, block):
    return jnp.concatenate([flipped[block], flipped[block + 1]], axis=1)


def first_mask(start, low_block):
    key_pos = lax.broadcasted_iota(jnp.int32, (256, 256), 0)
    row_pos = lax.broadcasted_iota(jnp.int32, (256, 256), 1) % BLOCK + BLOCK
    return (key_pos <= row_pos) & (key_pos >= (start - low_block) * BLOCK)


def later_mask(start, low_block):
    key_pos = lax.broadcasted_iota(jnp.int32, (256, 256), 0)
    return key_pos >= (start - low_block) * BLOCK


def heads_flipped(block):
    return jnp.concatenate([block[:, :HD].T, block[:, HD:].T], axis=1)


def heads_stacked(block):
    return jnp.concatenate([block[:, :HD], block[:, HD:]], axis=0)


def forward_kernel(
    table, q_ref, kv, far, near_own, near_far, att_ref, att_t_ref, total_ref, keys, values, values_t, sems
):
    b = pl.program_id(0)

    @pl.when(b == 0)
    def _():
        fill_pool(table, kv, far, near_own, near_far, keys, values, sems)
        transposed_pool(values, values_t)

    start = jnp.maximum(table[START + b], 0)
    diag = PRIOR + b
    steps = (diag - start) // 2 + 1

    def scores(step, q_t):
        low_block = diag - 1 - 2 * step
        low = pl.multiple_of(low_block * BLOCK, BLOCK)
        return low_block, dot(keys[pl.ds(low, 256), :], q_t) * SCALE_LOG2

    for pair in range(PAIRS):
        cols = slice(pair * 256, (pair + 1) * 256)
        q_t = heads_flipped(q_ref[:, cols])
        low_block, s = scores(0, q_t)
        s = jnp.where(first_mask(start, low_block), s, MASKED)
        top = jnp.max(s, axis=0, keepdims=True)
        p = jnp.exp2(s - top)
        total = jnp.sum(p, axis=0, keepdims=True)
        acc = dot(pair_of(values_t, low_block), p.astype(jnp.bfloat16))

        def body(step, carry):
            top, total, acc = carry
            low_block, s = scores(step, q_t)
            s = jnp.where(later_mask(start, low_block), s, MASKED)
            top_new = jnp.maximum(top, jnp.max(s, axis=0, keepdims=True))
            fade = jnp.exp2(top - top_new)
            p = jnp.exp2(s - top_new)
            total = total * fade + jnp.sum(p, axis=0, keepdims=True)
            acc = acc * fade + dot(pair_of(values_t, low_block), p.astype(jnp.bfloat16))
            return top_new, total, acc

        top, total, acc = lax.fori_loop(1, steps, body, (top, total, acc))
        out = acc * (1.0 / total)
        att_t_ref[0, :, cols] = out.astype(jnp.bfloat16)
        for head in range(2):
            at = pair * 256 + head * HD
            att_ref[:, at : at + HD] = out[:, head * HD : (head + 1) * HD].T.astype(jnp.bfloat16)
        total_ref[0, :, cols] = top + jnp.log2(total)


def forward(table, queries, kv, far, near_own, near_far, chunk):
    return pl.pallas_call(
        forward_kernel,
        grid=(BLK_DEV,),
        in_specs=[SMEM, pl.BlockSpec((BLOCK, CW), lambda b: (b, chunk)), ANY, ANY, ANY, ANY],
        out_specs=[
            pl.BlockSpec((BLOCK, CW), lambda b: (b, 0)),
            pl.BlockSpec((1, HD, CW), lambda b: (b, 0, 0)),
            pl.BlockSpec((1, 1, CW), lambda b: (b, 0, 0)),
        ],
        out_shape=[
            jax.ShapeDtypeStruct((ROWS, CW), jnp.bfloat16),
            jax.ShapeDtypeStruct((BLK_DEV, HD, CW), jnp.bfloat16),
            jax.ShapeDtypeStruct((BLK_DEV, 1, CW), jnp.float32),
        ],
        scratch_shapes=[
            pltpu.VMEM((POOL * BLOCK, HD), jnp.bfloat16),
            pltpu.VMEM((POOL * BLOCK, HD), jnp.bfloat16),
            pltpu.VMEM((POOL, HD, BLOCK), jnp.bfloat16),
            pltpu.SemaphoreType.DMA((6,)),
        ],
        compiler_params=params(),
        name="attention_forward",
    )(table, queries, kv, far, near_own, near_far)


def start_chosen(rel, index, sources, place, sem, col=0):
    for at, source in enumerate(sources):
        @pl.when(rel == at)
        def _():
            pltpu.make_async_copy(
                source.at[pl.ds(pl.multiple_of(index * BLOCK, BLOCK), BLOCK)], place, sem
            ).start()


def backward_kernel(last, first, *refs):
    refs = list(refs)
    table, q_ref, att_t_ref, total_ref, kv, far, near_own, near_far = refs[:8]
    sources = refs[8:12]
    refs = refs[12:]
    if not first:
        key_in, value_in = refs[:2]
        refs = refs[2:]
    dq_ref = refs[0]
    if last:
        own_ref, near_ref, far_ref = refs[1:4]
        refs = refs[4:]
    else:
        key_out, value_out = refs[1:3]
        refs = refs[3:]
    keys, values, keys_t, grads, key_acc, value_acc, sems, grad_sems = refs
    b = pl.program_id(0)

    def grad_place(at):
        return grads.at[pl.ds(at * BLOCK, BLOCK)]

    @pl.when(b == 0)
    def _():
        for at in range(BLK_DEV):
            start_chosen(
                table[GRAD_REL + at], table[GRAD_IDX + at], sources, grad_place(at), grad_sems.at[at]
            )
        if first:
            key_acc[...] = jnp.zeros_like(key_acc)
            value_acc[...] = jnp.zeros_like(value_acc)
        else:
            key_acc[...] = key_in[...]
            value_acc[...] = value_in[...]
        fill_pool(table, kv, far, near_own, near_far, keys, values, sems)
        transposed_pool(keys, keys_t)
        for at in range(BLK_DEV):
            pltpu.make_async_copy(
                sources[0].at[pl.ds(0, BLOCK)], grad_place(at), grad_sems.at[at]
            ).wait()

    start = jnp.maximum(table[START + b], 0)
    diag = PRIOR + b
    steps = (diag - start) // 2 + 1
    grad_row = pl.multiple_of(b * BLOCK, BLOCK)

    for pair in range(PAIRS):
        cols = slice(pair * 256, (pair + 1) * 256)
        q = q_ref[:, cols]
        q_t = heads_flipped(q)
        q_s = heads_stacked(q)
        g = grads[pl.ds(grad_row, BLOCK), cols]
        g_t = heads_flipped(g)
        g_s = heads_stacked(g)
        delta = jnp.sum(
            g_t.astype(jnp.float32) * att_t_ref[0, :, cols].astype(jnp.float32),
            axis=0,
            keepdims=True,
        )
        log_total = total_ref[0, :, cols]

        def tile(step, mask):
            low_block = diag - 1 - 2 * step
            low = pl.multiple_of(low_block * BLOCK, BLOCK)
            k = keys[pl.ds(low, 256), :]
            v = values[pl.ds(low, 256), :]
            s = dot(k, q_t) * SCALE_LOG2
            s = jnp.where(mask(start, low_block), s, MASKED)
            p = jnp.exp2(s - log_total).astype(jnp.bfloat16)
            dp = dot(v, g_t)
            ds = (p.astype(jnp.float32) * (dp - delta)).astype(jnp.bfloat16)
            value_acc[pl.ds(low, 256), :] += dot(p, g_s)
            key_acc[pl.ds(low, 256), :] += dot(ds, q_s)
            return dot(pair_of(keys_t, low_block), ds)

        dq_t = tile(0, first_mask)
        dq_t = lax.fori_loop(1, steps, lambda step, acc: acc + tile(step, later_mask), dq_t)
        dq_t = dq_t * SCALE
        for head in range(2):
            at = pair * 256 + head * HD
            dq_ref[:, at : at + HD] = dq_t[:, head * HD : (head + 1) * HD].T.astype(jnp.bfloat16)

    @pl.when(b == BLK_DEV - 1)
    def _():
        if last:
            near_at = ROWS - BLOCK
            own_at = PRIOR * BLOCK
            own_ref[:ROWS] = key_acc[own_at:] * SCALE
            own_ref[ROWS:] = value_acc[own_at:]
            near_ref[:ROWS] = (key_acc[near_at:own_at] * SCALE).astype(jnp.bfloat16)
            near_ref[ROWS:] = value_acc[near_at:own_at].astype(jnp.bfloat16)
            empty = jnp.zeros((BLOCK, HD), jnp.bfloat16)
            far_ref[:BLOCK] = empty
            far_ref[BLOCK:ROWS] = (key_acc[:near_at] * SCALE).astype(jnp.bfloat16)
            far_ref[ROWS : ROWS + BLOCK] = empty
            far_ref[ROWS + BLOCK :] = value_acc[:near_at].astype(jnp.bfloat16)
        else:
            key_out[...] = key_acc[...]
            value_out[...] = value_acc[...]


def backward(table, queries, att_t, totals, pool, sources, carried, chunk, last):
    first = carried is None
    whole = lambda shape: pl.BlockSpec(shape, lambda b: (0,) * len(shape))
    pool_shape = (POOL * BLOCK, HD)
    in_specs = [
        SMEM,
        pl.BlockSpec((BLOCK, CW), lambda b: (b, chunk)),
        pl.BlockSpec((1, HD, CW), lambda b: (b, 0, 0)),
        pl.BlockSpec((1, 1, CW), lambda b: (b, 0, 0)),
    ] + [ANY] * 8
    if not first:
        in_specs += [whole(pool_shape)] * 2
    out_specs = [pl.BlockSpec((BLOCK, CW), lambda b: (b, 0))]
    out_shape = [jax.ShapeDtypeStruct((ROWS, CW), jnp.bfloat16)]
    if last:
        out_specs += [whole((2 * ROWS, HD))] * 3
        out_shape += [
            jax.ShapeDtypeStruct((2 * ROWS, HD), jnp.float32),
            jax.ShapeDtypeStruct((2 * ROWS, HD), jnp.bfloat16),
            jax.ShapeDtypeStruct((2 * ROWS, HD), jnp.bfloat16),
        ]
    else:
        out_specs += [whole(pool_shape)] * 2
        out_shape += [jax.ShapeDtypeStruct(pool_shape, jnp.float32)] * 2

    def kernel(*refs):
        backward_kernel(last, first, *refs)

    return pl.pallas_call(
        kernel,
        grid=(BLK_DEV,),
        in_specs=in_specs,
        out_specs=out_specs,
        out_shape=out_shape,
        scratch_shapes=[
            pltpu.VMEM(pool_shape, jnp.bfloat16),
            pltpu.VMEM(pool_shape, jnp.bfloat16),
            pltpu.VMEM((POOL, HD, BLOCK), jnp.bfloat16),
            pltpu.VMEM((ROWS, CW), jnp.bfloat16),
            pltpu.VMEM(pool_shape, jnp.float32),
            pltpu.VMEM(pool_shape, jnp.float32),
            pltpu.SemaphoreType.DMA((6,)),
            pltpu.SemaphoreType.DMA((BLK_DEV,)),
        ],
        compiler_params=params(),
        name="attention_backward",
    )(table, queries, att_t, totals, *pool, *sources, *([] if first else carried))


def grad_matmul_kernel(table, *refs):
    pieces, weight, outs = refs[:8], refs[8], refs[9:]
    j = pl.program_id(0)
    per_out = CW // 256
    for half in range(2):
        total = None
        for ahead in range(4):
            at = pl.multiple_of(((table[TP] + ahead) % 4) * WIDTH, WIDTH)
            term = dot_nt(pieces[2 * ahead + half][...], weight[:, pl.ds(at, WIDTH)])
            total = term if total is None else total + term
        value = total.astype(jnp.bfloat16)
        for c in range(CHUNKS):
            @pl.when(j // per_out == c)
            def _():
                outs[c][half * 256 : (half + 1) * 256, :] = value


def grad_matmul(table, pieces, weight):
    per_out = CW // 256

    def out_spec(c):
        return pl.BlockSpec(
            (ROWS, 256), lambda j, table: (0, jnp.clip(j - c * per_out, 0, per_out - 1))
        )

    return pl.pallas_call(
        grad_matmul_kernel,
        grid_spec=pltpu.PrefetchScalarGridSpec(
            num_scalar_prefetch=1,
            grid=(4,),
            in_specs=[pl.BlockSpec((ROWS // 2, WIDTH), lambda j, table: (0, 0))] * 8
            + [pl.BlockSpec((256, 4 * WIDTH), lambda j, table: (j, 0))],
            out_specs=[out_spec(c) for c in range(CHUNKS)],
        ),
        out_shape=[jax.ShapeDtypeStruct((ROWS, CW), jnp.bfloat16)] * CHUNKS,
        compiler_params=params(),
        name="grad_projection",
    )(table, *pieces, weight)


def far_product_kernel(table, *refs):
    sources = [refs[4 * c : 4 * c + 4] for c in range(CHUNKS)]
    weight, left, right, rows_out, rows, sems = refs[4 * CHUNKS :]
    j = pl.program_id(0)

    @pl.when(j == 0)
    def _():
        def place(c, at):
            return rows.at[pl.ds(at * BLOCK, BLOCK), pl.ds(c * CW, CW)]

        for c in range(CHUNKS):
            for at in range(BLK_DEV):
                start_chosen(
                    table[ATT_REL + at],
                    table[ATT_IDX + at],
                    sources[c],
                    place(c, at),
                    sems.at[c * BLK_DEV + at],
                )
        for c in range(CHUNKS):
            for at in range(BLK_DEV):
                pltpu.make_async_copy(
                    sources[c][0].at[pl.ds(0, BLOCK)], place(c, at), sems.at[c * BLK_DEV + at]
                ).wait()
        rows_out[...] = rows[...]

    value = dot(rows[...], weight[...]).astype(jnp.bfloat16)

    @pl.when(j < 2)
    def _():
        left[...] = value

    @pl.when(j >= 2)
    def _():
        right[...] = value


def far_product(table, sources, weight):
    flat = [source for group in sources for source in group]
    return pl.pallas_call(
        far_product_kernel,
        grid_spec=pltpu.PrefetchScalarGridSpec(
            num_scalar_prefetch=1,
            grid=(4,),
            in_specs=[ANY] * (4 * CHUNKS)
            + [pl.BlockSpec((WIDTH, 256), lambda j, table: (0, ((table[TP] + 2) % 4) * 4 + j))],
            out_specs=[
                pl.BlockSpec((ROWS, 256), lambda j, table: (0, jnp.minimum(j, 1))),
                pl.BlockSpec((ROWS, 256), lambda j, table: (0, jnp.maximum(j - 2, 0))),
                pl.BlockSpec((ROWS, WIDTH), lambda j, table: (0, 0)),
            ],
            scratch_shapes=[
                pltpu.VMEM((ROWS, WIDTH), jnp.bfloat16),
                pltpu.SemaphoreType.DMA((4 * CHUNKS,)),
            ],
        ),
        out_shape=[jax.ShapeDtypeStruct((ROWS, 512), jnp.bfloat16)] * 2
        + [jax.ShapeDtypeStruct((ROWS, WIDTH), jnp.bfloat16)],
        compiler_params=params(),
        name="far_product",
    )(table, *flat, weight)


def side_block(table, j, first_half):
    ahead = jnp.where(j < 2, 1, 3)
    half = jnp.where(j < 2, first_half, 1 - first_half)
    return ((table[TP] + ahead) % 4) * 4 + half * 2 + j % 2


def near_product_kernel(table, rows, weight, onward, back):
    value = dot(rows[...], weight[...]).astype(jnp.bfloat16)
    j = pl.program_id(0)

    @pl.when(j < 2)
    def _():
        onward[...] = value

    @pl.when(j >= 2)
    def _():
        back[...] = value


def sum_product_kernel(table, rows, weight, from_before, from_after, onward, back):
    value = dot(rows[...], weight[...])
    j = pl.program_id(0)

    @pl.when(j < 2)
    def _():
        onward[...] = (value + from_before[...].astype(jnp.float32)).astype(jnp.bfloat16)

    @pl.when(j >= 2)
    def _():
        back[...] = (value + from_after[...].astype(jnp.float32)).astype(jnp.bfloat16)


def side_products(table, rows, weight, received, first_half):
    front = pl.BlockSpec((ROWS, 256), lambda j, table: (0, jnp.minimum(j, 1)))
    rear = pl.BlockSpec((ROWS, 256), lambda j, table: (0, jnp.maximum(j - 2, 0)))
    return pl.pallas_call(
        near_product_kernel if received is None else sum_product_kernel,
        grid_spec=pltpu.PrefetchScalarGridSpec(
            num_scalar_prefetch=1,
            grid=(4,),
            in_specs=[
                pl.BlockSpec((ROWS, WIDTH), lambda j, table: (0, 0)),
                pl.BlockSpec((WIDTH, 256), lambda j, table: (0, side_block(table, j, first_half))),
            ]
            + ([] if received is None else [front, rear]),
            out_specs=[front, rear],
        ),
        out_shape=[jax.ShapeDtypeStruct((ROWS, 512), jnp.bfloat16)] * 2,
        compiler_params=params(),
        name="side_products",
    )(table, rows, weight, *([] if received is None else received))


def own_product_kernel(table, rows, weight, out):
    out[...] = dot(rows[...], weight[...])


def own_product(table, rows, weight):
    return pl.pallas_call(
        own_product_kernel,
        grid_spec=pltpu.PrefetchScalarGridSpec(
            num_scalar_prefetch=1,
            grid=(4,),
            in_specs=[
                pl.BlockSpec((ROWS, WIDTH), lambda j, table: (0, 0)),
                pl.BlockSpec((WIDTH, 256), lambda j, table: (0, table[TP] * 4 + j)),
            ],
            out_specs=pl.BlockSpec((ROWS, 256), lambda j, table: (0, j)),
        ),
        out_shape=jax.ShapeDtypeStruct((ROWS, WIDTH), jnp.float32),
        compiler_params=params(),
        name="own_product",
    )(table, rows, weight)


def last_sum_kernel(own, before_a, before_b, after_a, after_b, out):
    for half, before, after in ((0, before_a, after_a), (1, before_b, after_b)):
        cols = slice(half * 512, (half + 1) * 512)
        out[:, cols] = (
            own[:, cols] + before[...].astype(jnp.float32) + after[...].astype(jnp.float32)
        ).astype(jnp.bfloat16)


def last_sum(own, before_a, before_b, after_a, after_b):
    part = pl.BlockSpec((BLOCK, 512), lambda j: (j, 0))
    full = pl.BlockSpec((BLOCK, WIDTH), lambda j: (j, 0))
    return pl.pallas_call(
        last_sum_kernel,
        grid=(4,),
        in_specs=[full, part, part, part, part],
        out_specs=full,
        out_shape=jax.ShapeDtypeStruct((ROWS, WIDTH), jnp.bfloat16),
        compiler_params=params(),
        name="last_sum",
    )(own, before_a, before_b, after_a, after_b)


def scalar_table(doc_start, balanced_source):
    device = lax.axis_index("cp")
    member = device % GROUP
    group_blocks = GROUP * BLK_DEV
    group_first = device // GROUP * group_blocks
    sources = lax.dynamic_slice_in_dim(balanced_source, group_first, group_blocks) - group_first
    slots = jnp.arange(group_blocks, dtype=jnp.int32)
    slot_of = jnp.sum(
        jnp.where(sources[None, :] == slots[:, None], slots[None, :], 0), axis=1, dtype=jnp.int32
    )
    mine = member * BLK_DEV
    wanted = lax.dynamic_slice_in_dim(sources, mine, BLK_DEV)
    held = lax.dynamic_slice_in_dim(slot_of, mine, BLK_DEV)
    starts = lax.dynamic_slice_in_dim(doc_start, device * BLK_DEV, BLK_DEV)
    starts = starts - (device * BLK_DEV - PRIOR)
    return jnp.concatenate(
        [
            starts,
            (held // BLK_DEV) ^ member,
            held % BLK_DEV,
            (wanted // BLK_DEV) ^ member,
            wanted % BLK_DEV,
            jnp.stack([device % 2, lax.axis_index("tp")]),
        ]
    ).astype(jnp.int32)


def group_exchange(block):
    across = swap_cp(block, 2)
    return [block, swap_cp(block, 1), across, swap_cp(across, 1)]


def shards(queries, key_rows, value_rows, out_proj, grad_mixed, doc_start, balanced_source):
    table = scalar_table(doc_start, balanced_source)

    kv = jnp.concatenate([key_rows, value_rows], axis=0)
    far = shift_cp(kv, 2)
    near_own = swap_cp(kv, 1)
    near_far = swap_cp(far, 1)
    pool = (kv, far, near_own, near_far)

    half = ROWS // 2
    upper, lower = grad_mixed[:half], grad_mixed[half:]
    before_upper = shift_tp(upper, 1)
    after_lower = shift_tp(lower, -1)
    before_lower = shift_tp(lower, 1)
    after_upper = shift_tp(upper, -1)
    opposite_upper = shift_tp(before_upper, 1)
    opposite_lower = shift_tp(after_lower, -1)

    attended, attended_t, totals, exchanged = [], [], [], []
    for chunk in range(CHUNKS):
        att, att_t, total = forward(table, queries, *pool, chunk)
        attended_t.append(att_t)
        totals.append(total)
        exchanged.append(group_exchange(att))

    far_left, far_right, rows = far_product(table, exchanged, out_proj)
    from_before = shift_tp(far_left, 1)
    from_after = shift_tp(far_right, -1)
    onward_b, back_a = side_products(table, rows, out_proj, None, 1)
    before_b = shift_tp(onward_b, 1)
    after_a = shift_tp(back_a, -1)
    onward_a, back_b = side_products(table, rows, out_proj, (from_before, from_after), 0)
    before_a = shift_tp(onward_a, 1)
    after_b = shift_tp(back_b, -1)
    own = own_product(table, rows, out_proj)
    mixed = last_sum(own, before_a, before_b, after_a, after_b)

    pieces = [
        upper,
        lower,
        after_upper,
        after_lower,
        opposite_upper,
        opposite_lower,
        before_upper,
        before_lower,
    ]
    grad_attended = grad_matmul(table, pieces, out_proj)
    carried = None
    query_grads = []
    for chunk in range(CHUNKS):
        sources = group_exchange(grad_attended[chunk])
        outs = backward(
            table, queries, attended_t[chunk], totals[chunk], pool, sources, carried, chunk,
            chunk == CHUNKS - 1,
        )
        query_grads.append(outs[0])
        carried = outs[1:]
    query_grad = jnp.concatenate(query_grads, axis=1)
    own_grads, near_grads, far_grads = carried
    near_back = shift_cp(near_grads, -1)
    far_back = shift_cp(far_grads, -2)
    kv_grads = (
        own_grads + near_back.astype(jnp.float32) + far_back.astype(jnp.float32)
    ).astype(jnp.bfloat16)
    return (mixed, query_grad, kv_grads[:ROWS], kv_grads[ROWS:])


def solution(mesh):
    placed = (P("cp", "tp"), P("cp", "tp"), P("cp", "tp"), P("tp", None), P("cp", "tp"), P(), P())
    return jax.shard_map(
        shards,
        mesh=mesh,
        in_specs=placed,
        out_specs=(P("cp", "tp"),) * 4,
        check_vma=False,
    )
```

```python
import math

import jax
import jax.numpy as jnp
from jax import lax
from jax.experimental import pallas as pl
from jax.experimental.pallas import tpu as pltpu
from jax.sharding import PartitionSpec as P

HD = 128
BLOCK = 128
BLK_DEV = 4
MAXB = 8
GROUP = 4
PRIOR = MAXB - 1
POOL = PRIOR + BLK_DEV
ROWS = BLOCK * BLK_DEV
WIDTH = 1024
FAR_ROWS = (PRIOR - BLK_DEV) * BLOCK
CHUNKS = 2
CW = WIDTH // CHUNKS
FW = 512
BW = 512

SCALE = 1.0 / math.sqrt(HD)
SCALE_LOG2 = SCALE * math.log2(math.e)
MASKED = -1e30

START, GRAD_REL, GRAD_IDX, ATT_REL, ATT_IDX, CORE, TP = 0, 4, 8, 12, 16, 20, 21

ANY = pl.BlockSpec(memory_space=pl.ANY)
WHOLE = pl.BlockSpec(memory_space=pltpu.VMEM)
HBM = pl.BlockSpec(memory_space=pltpu.HBM)
SMEM = pl.BlockSpec(memory_space=pltpu.SMEM)
VMEM_LIMIT = 48 * 1024 * 1024


PARAMS = pltpu.CompilerParams(vmem_limit_bytes=VMEM_LIMIT)


def lasting(us):
    return pl.CostEstimate(
        flops=int(us * 1.15e9), bytes_accessed=int(us * 3.6e6), transcendentals=0
    )


def dot(a, b):
    return jnp.dot(a, b, preferred_element_type=jnp.float32)


def dot_nt(a, b):
    return lax.dot_general(a, b, (((1,), (1,)), ((), ())), preferred_element_type=jnp.float32)


def swap_cp(block, mask):
    count = lax.axis_size("cp")
    return lax.ppermute(block, "cp", [(i, i ^ mask) for i in range(count)])


def shift_cp(block, distance):
    count = lax.axis_size("cp")
    route = [(i, i + distance) for i in range(count) if 0 <= i + distance < count]
    return lax.ppermute(block, "cp", route)


def shift_tp(block, distance):
    count = lax.axis_size("tp")
    return lax.ppermute(block, "tp", [(i, (i + distance) % count) for i in range(count)])


def pool_copies(kv, far, near, keys, values, sems):
    copies = []
    for src, row, rows, place in (
        (kv, 0, ROWS, PRIOR * BLOCK),
        (far, 0, FAR_ROWS, 0),
        (near, 0, ROWS, ROWS - BLOCK),
    ):
        for col, pool in ((0, keys), (HD, values)):
            copies.append(
                pltpu.make_async_copy(
                    src.at[pl.ds(row, rows), pl.ds(col, HD)],
                    pool.at[pl.ds(place, rows)],
                    sems.at[len(copies)],
                )
            )
    return copies


def block_rows(b):
    return pl.ds(pl.multiple_of(b * BLOCK, BLOCK), BLOCK)


def first_mask(odd, width):
    key_pos = lax.broadcasted_iota(jnp.int32, (256, width), 0)
    row_pos = lax.broadcasted_iota(jnp.int32, (256, width), 1) % BLOCK + BLOCK
    return (key_pos <= row_pos) & (key_pos >= odd * BLOCK)


def flipped_heads(block):
    heads = block.shape[1] // HD
    return jnp.concatenate([block[:, h * HD : (h + 1) * HD].T for h in range(heads)], axis=1)


def stacked_heads(block):
    heads = block.shape[1] // HD
    return jnp.concatenate([block[:, h * HD : (h + 1) * HD] for h in range(heads)], axis=0)


def tiles_of(table, b):
    diag = PRIOR + b
    count = diag - jnp.maximum(table[START + b], 0) + 1
    return (count + 1) // 2, count % 2, diag


def low_of(step, odd, diag):
    block = diag - 1 - 2 * step + jnp.where(step > 0, odd, 0)
    return pl.multiple_of(block * BLOCK, BLOCK)


def forward_kernel(
    chunk, table, q_hbm, kv, far, near, att_hbm, att_t_hbm, total_ref,
    keys, values, q_ref, att, att_t, sems, out_sems,
):
    copies = [pltpu.make_async_copy(q_hbm.at[:, pl.ds(chunk * CW, CW)], q_ref, sems.at[6])]
    copies += pool_copies(kv, far, near, keys, values, sems)
    for copy in copies:
        copy.start()
    for copy in copies:
        copy.wait()

    def outward(b):
        return [
            pltpu.make_async_copy(att.at[block_rows(b)], att_hbm.at[block_rows(b)], out_sems.at[b]),
            pltpu.make_async_copy(att_t.at[b], att_t_hbm.at[b], out_sems.at[BLK_DEV + b]),
        ]

    groups = [slice(at, at + FW) for at in range(0, CW, FW)]

    def block(b, _):
        steps, odd, diag = tiles_of(table, b)
        q_t = [flipped_heads(q_ref[block_rows(b), cols]) for cols in groups]

        def tile(step, mask, carry):
            low = low_of(step, odd, diag)
            k = keys[pl.ds(low, 256), :]
            v_t = values[pl.ds(low, 256), :].T
            result = []
            for at in range(len(groups)):
                s = dot(k, q_t[at]) * SCALE_LOG2
                if carry is None:
                    s = jnp.where(mask, s, MASKED)
                    top = jnp.max(s, axis=0, keepdims=True)
                    p = jnp.exp2(s - top)
                    total = jnp.sum(p, axis=0, keepdims=True)
                    acc = dot(v_t, p.astype(jnp.bfloat16))
                else:
                    top_old, total, acc = carry[at]
                    top = jnp.maximum(top_old, jnp.max(s, axis=0, keepdims=True))
                    fade = jnp.exp2(top_old - top)
                    p = jnp.exp2(s - top)
                    total = total * fade + jnp.sum(p, axis=0, keepdims=True)
                    acc = acc * fade + dot(v_t, p.astype(jnp.bfloat16))
                result.append((top, total, acc))
            return result

        carry = tile(0, first_mask(odd, FW), None)
        carry = lax.fori_loop(1, steps, lambda step, carry: tile(step, None, carry), carry)
        for cols, (top, total, acc) in zip(groups, carry):
            out = (acc * (1.0 / total)).astype(jnp.bfloat16)
            att_t[b, :, cols] = out
            for head in range(FW // HD):
                at = cols.start + head * HD
                att[block_rows(b), at : at + HD] = out[:, head * HD : (head + 1) * HD].T
            total_ref[b, :, cols] = top + jnp.log2(total)
        for copy in outward(b):
            copy.start()
        return _

    lax.fori_loop(0, BLK_DEV, block, 0)
    for b in range(BLK_DEV):
        for copy in outward(b):
            copy.wait()


def forward(table, queries, kv, far, near, chunk):
    def kernel(*refs):
        forward_kernel(chunk, *refs)

    return pl.pallas_call(
        kernel,
        in_specs=[SMEM] + [ANY] * 4,
        out_specs=[ANY, ANY, WHOLE],
        out_shape=[
            jax.ShapeDtypeStruct((ROWS, CW), jnp.bfloat16),
            jax.ShapeDtypeStruct((BLK_DEV, HD, CW), jnp.bfloat16),
            jax.ShapeDtypeStruct((BLK_DEV, 1, CW), jnp.float32),
        ],
        scratch_shapes=[
            pltpu.VMEM((POOL * BLOCK, HD), jnp.bfloat16),
            pltpu.VMEM((POOL * BLOCK, HD), jnp.bfloat16),
            pltpu.VMEM((ROWS, CW), jnp.bfloat16),
            pltpu.VMEM((ROWS, CW), jnp.bfloat16),
            pltpu.VMEM((BLK_DEV, HD, CW), jnp.bfloat16),
            pltpu.SemaphoreType.DMA((7,)),
            pltpu.SemaphoreType.DMA((2 * BLK_DEV,)),
        ],
        compiler_params=PARAMS,
        cost_estimate=lasting(8),
        name="attention_forward",
    )(table, queries, kv, far, near)


def start_chosen(rel, index, sources, place, sem, col=0):
    for at, source in enumerate(sources):
        @pl.when(rel == at)
        def _():
            pltpu.make_async_copy(
                source.at[pl.ds(pl.multiple_of(index * BLOCK, BLOCK), BLOCK)], place, sem
            ).start()


def backward_kernel(chunk, last, first, *refs):
    refs = list(refs)
    table, q_hbm, att_t_hbm, total_ref, kv, far, near = refs[:7]
    sources = refs[7:11]
    refs = refs[11:]
    if not first:
        key_in, value_in = refs[1:3]
        refs = refs[3:]
    dq_hbm = refs[0]
    if last:
        own_ref, near_ref, far_ref = refs[1:4]
        refs = refs[4:]
        key_acc, value_acc = refs[:2]
    else:
        key_acc, value_acc = refs[1:3]
        refs = refs[3:]
    keys, values, q_ref, att_t, grads, dq, sems, grad_sems, out_sems = refs[-9:]

    incoming = [
        pltpu.make_async_copy(q_hbm.at[:, pl.ds(chunk * CW, CW)], q_ref, sems.at[6]),
        pltpu.make_async_copy(att_t_hbm, att_t, sems.at[7]),
    ]
    if not first:
        incoming += [
            pltpu.make_async_copy(key_in, key_acc, sems.at[8]),
            pltpu.make_async_copy(value_in, value_acc, sems.at[9]),
        ]
    incoming += pool_copies(kv, far, near, keys, values, sems)
    for at in range(BLK_DEV):
        start_chosen(
            table[GRAD_REL + at], table[GRAD_IDX + at], sources, grads.at[block_rows(at)], grad_sems.at[at]
        )
    for copy in incoming:
        copy.start()
    if first:
        key_acc[...] = jnp.zeros_like(key_acc)
        value_acc[...] = jnp.zeros_like(value_acc)
    for copy in incoming:
        copy.wait()
    for at in range(BLK_DEV):
        pltpu.make_async_copy(
            sources[0].at[pl.ds(0, BLOCK)], grads.at[block_rows(at)], grad_sems.at[at]
        ).wait()

    def outward(b):
        return pltpu.make_async_copy(
            dq.at[block_rows(b)], dq_hbm.at[block_rows(b), pl.ds(chunk * CW, CW)], out_sems.at[b]
        )

    groups = [slice(at, at + BW) for at in range(0, CW, BW)]

    def block(b, _):
        steps, odd, diag = tiles_of(table, b)
        held = []
        for cols in groups:
            q = q_ref[block_rows(b), cols]
            g = grads[block_rows(b), cols]
            g_t = flipped_heads(g)
            delta = jnp.sum(
                g_t.astype(jnp.float32) * att_t[b, :, cols].astype(jnp.float32),
                axis=0,
                keepdims=True,
            )
            held.append(
                (flipped_heads(q), stacked_heads(q), g_t, stacked_heads(g), delta, total_ref[b, :, cols])
            )

        def tile(step, mask, carry):
            low = low_of(step, odd, diag)
            k = keys[pl.ds(low, 256), :]
            k_t = k.T
            v = values[pl.ds(low, 256), :]
            result = []
            key_part = value_part = None
            for at, (q_t, q_s, g_t, g_s, delta, log_total) in enumerate(held):
                s = dot(k, q_t) * SCALE_LOG2
                if mask is not None:
                    s = jnp.where(mask, s, MASKED)
                p = jnp.exp2(s - log_total).astype(jnp.bfloat16)
                dp = dot(v, g_t)
                ds = (p.astype(jnp.float32) * (dp - delta)).astype(jnp.bfloat16)
                value_term, key_term, query_term = dot(p, g_s), dot(ds, q_s), dot(k_t, ds)
                value_part = value_term if value_part is None else value_part + value_term
                key_part = key_term if key_part is None else key_part + key_term
                result.append(query_term if carry is None else carry[at] + query_term)
            value_acc[pl.ds(low, 256), :] += value_part
            key_acc[pl.ds(low, 256), :] += key_part
            return result

        carry = tile(0, first_mask(odd, BW), None)
        carry = lax.fori_loop(1, steps, lambda step, carry: tile(step, None, carry), carry)
        for cols, dq_t in zip(groups, carry):
            dq_t = (dq_t * SCALE).astype(jnp.bfloat16)
            for head in range(BW // HD):
                at = cols.start + head * HD
                dq[block_rows(b), at : at + HD] = dq_t[:, head * HD : (head + 1) * HD].T
        outward(b).start()
        return _

    lax.fori_loop(0, BLK_DEV, block, 0)

    if last:
        near_at = ROWS - BLOCK
        own_at = PRIOR * BLOCK
        for acc, cols, factor in ((key_acc, slice(0, HD), SCALE), (value_acc, slice(HD, 2 * HD), 1.0)):
            own_ref[:, cols] = acc[own_at:] * factor
            near_ref[:, cols] = (acc[near_at:own_at] * factor).astype(jnp.bfloat16)
            far_ref[:, cols] = (acc[:near_at] * factor).astype(jnp.bfloat16)
    for b in range(BLK_DEV):
        outward(b).wait()


def backward(table, queries, att_t, totals, pool, sources, carried, chunk, last):
    first = carried is None
    pool_shape = (POOL * BLOCK, HD)
    sums = [jax.ShapeDtypeStruct(pool_shape, jnp.float32)] * 2
    if last:
        out_shape = [
            jax.ShapeDtypeStruct((ROWS, 2 * HD), jnp.float32),
            jax.ShapeDtypeStruct((ROWS, 2 * HD), jnp.bfloat16),
            jax.ShapeDtypeStruct((FAR_ROWS, 2 * HD), jnp.bfloat16),
        ]
        scratch = [pltpu.VMEM(pool_shape, jnp.float32)] * 2
    else:
        out_shape, scratch = sums, []

    def kernel(*refs):
        backward_kernel(chunk, last, first, *refs)

    return pl.pallas_call(
        kernel,
        in_specs=[SMEM, ANY, ANY, WHOLE] + [ANY] * (7 if first else 10),
        out_specs=[ANY] + [WHOLE] * len(out_shape),
        out_shape=[jax.ShapeDtypeStruct((ROWS, WIDTH), jnp.bfloat16)] + out_shape,
        input_output_aliases={} if first else {11: 0},
        scratch_shapes=scratch
        + [
            pltpu.VMEM(pool_shape, jnp.bfloat16),
            pltpu.VMEM(pool_shape, jnp.bfloat16),
            pltpu.VMEM((ROWS, CW), jnp.bfloat16),
            pltpu.VMEM((BLK_DEV, HD, CW), jnp.bfloat16),
            pltpu.VMEM((ROWS, CW), jnp.bfloat16),
            pltpu.VMEM((ROWS, CW), jnp.bfloat16),
            pltpu.SemaphoreType.DMA((10,)),
            pltpu.SemaphoreType.DMA((BLK_DEV,)),
            pltpu.SemaphoreType.DMA((BLK_DEV,)),
        ],
        compiler_params=PARAMS,
        cost_estimate=lasting(9),
        name="attention_backward",
    )(table, queries, att_t, totals, *pool, *sources, *([] if first else carried))


def grad_matmul_kernel(chunk, table, *refs):
    pieces, weight_hbm, out, weight, sems = refs[:8], *refs[8:]
    half = ROWS // 2
    copies = []
    for ahead in range(4):
        at = pl.multiple_of(((table[TP] + ahead) % 4) * WIDTH, WIDTH)
        copies.append(
            pltpu.make_async_copy(
                weight_hbm.at[pl.ds(chunk * CW, CW), pl.ds(at, WIDTH)],
                weight.at[ahead],
                sems.at[ahead],
            )
        )
        copies[-1].start()
    totals = [None, None]
    for ahead in range(4):
        copies[ahead].wait()
        for part in range(2):
            term = dot_nt(pieces[2 * ahead + part][...], weight[ahead])
            totals[part] = term if totals[part] is None else totals[part] + term
    for part in range(2):
        out[part * half : (part + 1) * half] = totals[part].astype(jnp.bfloat16)


def grad_matmul(table, pieces, weight, chunk):
    def kernel(*refs):
        grad_matmul_kernel(chunk, *refs)

    return pl.pallas_call(
        kernel,
        in_specs=[SMEM] + [WHOLE] * 8 + [ANY],
        out_specs=WHOLE,
        out_shape=jax.ShapeDtypeStruct((ROWS, CW), jnp.bfloat16),
        scratch_shapes=[
            pltpu.VMEM((4, CW, WIDTH), jnp.bfloat16),
            pltpu.SemaphoreType.DMA((4,)),
        ],
        compiler_params=PARAMS,
        cost_estimate=lasting(4),
        name="grad_projection",
    )(table, *pieces, weight)


HALF = WIDTH // 2


def weight_copy(table, weight_hbm, weight, slot, ahead, half, sem):
    at = pl.multiple_of(((table[TP] + ahead) % 4) * WIDTH + half * HALF, HALF)
    return pltpu.make_async_copy(weight_hbm.at[:, pl.ds(at, HALF)], weight.at[slot], sem)


def product_kernel(table, *refs):
    sources = [refs[4 * c : 4 * c + 4] for c in range(CHUNKS)]
    weight_hbm, left, right, onward, back, own, rows, weight, sems, weight_sems = refs[4 * CHUNKS :]

    def place(c, at):
        return rows.at[block_rows(at), pl.ds(c * CW, CW)]

    places = [(c, at, c * BLK_DEV + at) for c in range(CHUNKS) for at in range(BLK_DEV)]
    for c, at, sem in places:
        start_chosen(
            table[ATT_REL + at], table[ATT_IDX + at], sources[c], place(c, at), sems.at[sem]
        )
    parts = ((2, 0), (2, 1), (1, 1), (3, 0), (0, 0), (0, 1))
    weights = [
        weight_copy(table, weight_hbm, weight, slot, ahead, half, weight_sems.at[slot])
        for slot, (ahead, half) in enumerate(parts)
    ]
    for copy in weights:
        copy.start()
    for c, at, sem in places:
        pltpu.make_async_copy(sources[c][0].at[pl.ds(0, BLOCK)], place(c, at), sems.at[sem]).wait()
    for slot, out in enumerate((left, right, onward, back)):
        weights[slot].wait()
        out[...] = dot(rows[...], weight[slot]).astype(jnp.bfloat16)
    for slot in (4, 5):
        weights[slot].wait()
        own[:, (slot - 4) * HALF : (slot - 3) * HALF] = dot(rows[...], weight[slot]).astype(
            jnp.bfloat16
        )


def products(table, sources, weight):
    flat = [source for group in sources for source in group]
    return pl.pallas_call(
        product_kernel,
        in_specs=[SMEM] + [ANY] * (4 * CHUNKS + 1),
        out_specs=[WHOLE] * 6,
        out_shape=[jax.ShapeDtypeStruct((ROWS, HALF), jnp.bfloat16)] * 4
        + [jax.ShapeDtypeStruct((ROWS, WIDTH), jnp.bfloat16)] * 2,
        scratch_shapes=[
            pltpu.VMEM((6, WIDTH, HALF), jnp.bfloat16),
            pltpu.SemaphoreType.DMA((4 * CHUNKS,)),
            pltpu.SemaphoreType.DMA((6,)),
        ],
        compiler_params=PARAMS,
        cost_estimate=lasting(7),
        name="products",
    )(table, *flat, weight)


def sum_product_kernel(table, rows, weight_hbm, before, after_, onward, back, weight, sems):
    weights = [
        weight_copy(table, weight_hbm, weight, 0, 1, 0, sems.at[0]),
        weight_copy(table, weight_hbm, weight, 1, 3, 1, sems.at[1]),
    ]
    for copy in weights:
        copy.start()
    for slot, (extra, out) in enumerate(((before, onward), (after_, back))):
        weights[slot].wait()
        value = dot(rows[...], weight[slot])
        out[...] = (value + extra[...].astype(jnp.float32)).astype(jnp.bfloat16)


def sum_products(table, rows, weight, before, after):
    half = jax.ShapeDtypeStruct((ROWS, HALF), jnp.bfloat16)
    return pl.pallas_call(
        sum_product_kernel,
        in_specs=[SMEM, WHOLE, ANY, WHOLE, WHOLE],
        out_specs=[WHOLE] * 2,
        out_shape=[half] * 2,
        scratch_shapes=[
            pltpu.VMEM((2, WIDTH, HALF), jnp.bfloat16),
            pltpu.SemaphoreType.DMA((2,)),
        ],
        compiler_params=PARAMS,
        cost_estimate=lasting(4),
        name="sum_products",
    )(table, rows, weight, before, after)


def last_sum_kernel(own, before_a, before_b, after_a, after_b, out):
    for half, before, after in ((0, before_a, after_a), (1, before_b, after_b)):
        cols = slice(half * 512, (half + 1) * 512)
        out[:, cols] = (
            own[:, cols].astype(jnp.float32) + before[...].astype(jnp.float32) + after[...].astype(jnp.float32)
        ).astype(jnp.bfloat16)


def last_sum(own, before_a, before_b, after_a, after_b):
    part = pl.BlockSpec((BLOCK, 512), lambda j: (j, 0))
    full = pl.BlockSpec((BLOCK, WIDTH), lambda j: (j, 0))
    return pl.pallas_call(
        last_sum_kernel,
        grid=(4,),
        in_specs=[full, part, part, part, part],
        out_specs=full,
        out_shape=jax.ShapeDtypeStruct((ROWS, WIDTH), jnp.bfloat16),
        compiler_params=PARAMS,
        cost_estimate=lasting(2),
        name="last_sum",
    )(own, before_a, before_b, after_a, after_b)


def scalar_table(doc_start, balanced_source):
    device = lax.axis_index("cp")
    member = device % GROUP
    group_blocks = GROUP * BLK_DEV
    group_first = device // GROUP * group_blocks
    sources = lax.dynamic_slice_in_dim(balanced_source, group_first, group_blocks) - group_first
    slots = jnp.arange(group_blocks, dtype=jnp.int32)
    slot_of = jnp.sum(
        jnp.where(sources[None, :] == slots[:, None], slots[None, :], 0), axis=1, dtype=jnp.int32
    )
    mine = member * BLK_DEV
    wanted = lax.dynamic_slice_in_dim(sources, mine, BLK_DEV)
    held = lax.dynamic_slice_in_dim(slot_of, mine, BLK_DEV)
    starts = lax.dynamic_slice_in_dim(doc_start, device * BLK_DEV, BLK_DEV)
    starts = starts - (device * BLK_DEV - PRIOR)
    return jnp.concatenate(
        [
            starts,
            (held // BLK_DEV) ^ member,
            held % BLK_DEV,
            (wanted // BLK_DEV) ^ member,
            wanted % BLK_DEV,
            jnp.stack([device % 2, lax.axis_index("tp")]),
        ]
    ).astype(jnp.int32)


def group_exchange(block, earlier):
    across = swap_cp(block, 2)
    return [block, swap_cp(after(block, earlier), 1), across, swap_cp(after(across, earlier), 1)]


def copy_all(*pairs, sems):
    copies = [pltpu.make_async_copy(src, dst, sems.at[at]) for at, (src, dst) in enumerate(pairs)]
    for copy in copies:
        copy.start()
    for copy in copies:
        copy.wait()


def join_kernel(keys, values, kv, last, sems):
    tail = pl.ds(ROWS - FAR_ROWS, FAR_ROWS)
    left, right = pl.ds(0, HD), pl.ds(HD, HD)
    copy_all(
        (keys, kv.at[:, left]),
        (values, kv.at[:, right]),
        (keys.at[tail], last.at[:, left]),
        (values.at[tail], last.at[:, right]),
        sems=sems,
    )


def join(keys, values):
    return pl.pallas_call(
        join_kernel,
        in_specs=[HBM] * 2,
        out_specs=[WHOLE] * 2,
        out_shape=[
            jax.ShapeDtypeStruct((ROWS, 2 * HD), jnp.bfloat16),
            jax.ShapeDtypeStruct((FAR_ROWS, 2 * HD), jnp.bfloat16),
        ],
        scratch_shapes=[pltpu.SemaphoreType.DMA((4,))],
        compiler_params=PARAMS,
        cost_estimate=lasting(2),
        name="join",
    )(keys, values)


def halve_kernel(grads, upper, lower, sems):
    half = ROWS // 2
    copy_all(
        (grads.at[pl.ds(0, half)], upper), (grads.at[pl.ds(half, half)], lower), sems=sems
    )


def halve(grads):
    return pl.pallas_call(
        halve_kernel,
        in_specs=[HBM],
        out_specs=[WHOLE] * 2,
        out_shape=[jax.ShapeDtypeStruct((ROWS // 2, WIDTH), jnp.bfloat16)] * 2,
        scratch_shapes=[pltpu.SemaphoreType.DMA((2,))],
        compiler_params=PARAMS,
        cost_estimate=lasting(2),
        name="halve",
    )(grads)


def add_kernel(own, near, far, keys, values):
    total = own[...] + near[...].astype(jnp.float32)
    front = total[: ROWS - FAR_ROWS].astype(jnp.bfloat16)
    rear = (total[ROWS - FAR_ROWS :] + far[...].astype(jnp.float32)).astype(jnp.bfloat16)
    for col, out in ((0, keys), (HD, values)):
        out[: ROWS - FAR_ROWS] = front[:, col : col + HD]
        out[ROWS - FAR_ROWS :] = rear[:, col : col + HD]


def add_terms(own, near, far):
    return pl.pallas_call(
        add_kernel,
        in_specs=[WHOLE] * 3,
        out_specs=[WHOLE] * 2,
        out_shape=[jax.ShapeDtypeStruct((ROWS, HD), jnp.bfloat16)] * 2,
        compiler_params=PARAMS,
        cost_estimate=lasting(1),
        name="add_terms",
    )(own, near, far)


def after(value, earlier):
    return lax.optimization_barrier((value, earlier))[0]


def shards(queries, key_rows, value_rows, out_proj, grad_mixed, doc_start, balanced_source):
    table = scalar_table(doc_start, balanced_source)

    kv, last = join(key_rows, value_rows)
    far = shift_cp(last, 2)
    near = shift_cp(kv, 1)
    pool = (kv, far, near)

    upper, lower = halve(after(grad_mixed, kv))
    before_upper = shift_tp(upper, 1)
    after_lower = shift_tp(lower, -1)
    before_lower = shift_tp(lower, 1)
    after_upper = shift_tp(upper, -1)

    attended, attended_t, totals = [], [], []
    for chunk in range(CHUNKS):
        att, att_t, total = forward(
            after(table, (attended[0], before_upper, after_lower, before_lower, after_upper))
            if chunk
            else table,
            queries,
            *pool,
            chunk,
        )
        attended.append(att)
        attended_t.append(att_t)
        totals.append(total)

    arrived = (attended[0], before_lower, after_upper)
    opposite_upper = shift_tp(after(before_upper, arrived), 1)
    opposite_lower = shift_tp(after(after_lower, arrived), -1)
    pieces = [
        upper,
        lower,
        after_upper,
        after_lower,
        opposite_upper,
        opposite_lower,
        before_upper,
        before_lower,
    ]
    exchanged = [group_exchange(attended[0], attended[1]), None]
    grad_attended = [grad_matmul(table, pieces, out_proj, 0), None]
    exchanged[1] = group_exchange(attended[1], grad_attended[0])
    grad_across = swap_cp(grad_attended[0], 2)
    grad_attended[1] = grad_matmul(after(table, grad_attended[0]), pieces, out_proj, 1)

    far_left, far_right, onward_b, back_a, own, rows = products(
        after(table, grad_attended[1]), exchanged, out_proj
    )
    from_before = shift_tp(far_left, 1)
    from_after = shift_tp(far_right, -1)

    grad_sources = [
        [
            grad_attended[0],
            swap_cp(after(grad_attended[0], own), 1),
            grad_across,
            swap_cp(after(grad_across, own), 1),
        ]
    ]
    carried = backward(
        after(table, own),
        queries, attended_t[0], totals[0], pool, grad_sources[0], None, 0, False,
    )
    query_a = carried[1]
    across = swap_cp(after(grad_attended[1], tuple(grad_sources[0])), 2)
    grad_sources.append(
        [
            grad_attended[1],
            swap_cp(after(grad_attended[1], query_a), 1),
            across,
            swap_cp(after(across, query_a), 1),
        ]
    )
    before_b = shift_tp(onward_b, 1)
    after_a = shift_tp(back_a, -1)
    onward_a, back_b = sum_products(after(table, query_a), rows, out_proj, from_before, from_after)
    before_a = shift_tp(onward_a, 1)
    after_b = shift_tp(back_b, -1)
    query_grad, own_grads, near_grads, far_grads = backward(
        after(table, onward_a),
        queries, attended_t[1], totals[1], pool, grad_sources[1], carried, 1, True,
    )
    far_back = shift_cp(after(far_grads, (before_b, after_a)), -2)
    near_back = shift_cp(after(near_grads, (before_b, after_a)), -1)
    mixed = last_sum(own, before_a, before_b, after_a, after_b)
    key_grad, value_grad = add_terms(after(own_grads, mixed), near_back, far_back)
    return (mixed, query_grad, key_grad, value_grad)


def solution(mesh):
    placed = (P("cp", "tp"), P("cp", "tp"), P("cp", "tp"), P("tp", None), P("cp", "tp"), P(), P())
    return jax.shard_map(
        shards,
        mesh=mesh,
        in_specs=placed,
        out_specs=(P("cp", "tp"),) * 4,
        check_vma=False,
    )
```

```python
import math

import jax
import jax.numpy as jnp
from jax import lax
from jax.experimental import pallas as pl
from jax.experimental.pallas import tpu as pltpu
from jax.sharding import PartitionSpec as P

HD = 128
BLOCK = 128
BLK_DEV = 4
MAXB = 8
GROUP = 4
PRIOR = MAXB - 1
POOL = PRIOR + BLK_DEV
ROWS = BLOCK * BLK_DEV
WIDTH = 1024
FAR_ROWS = (PRIOR - BLK_DEV) * BLOCK
CHUNKS = 2
CW = WIDTH // CHUNKS
FW = 512
BW = 512

SCALE = 1.0 / math.sqrt(HD)
SCALE_LOG2 = SCALE * math.log2(math.e)
MASKED = -1e30

START, GRAD_REL, GRAD_IDX, ATT_REL, ATT_IDX, CORE, TP = 0, 4, 8, 12, 16, 20, 21

ANY = pl.BlockSpec(memory_space=pl.ANY)
WHOLE = pl.BlockSpec(memory_space=pltpu.VMEM)
HBM = pl.BlockSpec(memory_space=pltpu.HBM)
SMEM = pl.BlockSpec(memory_space=pltpu.SMEM)
VMEM_LIMIT = 48 * 1024 * 1024


PARAMS = pltpu.CompilerParams(vmem_limit_bytes=VMEM_LIMIT)


def lasting(us):
    return pl.CostEstimate(
        flops=int(us * 1.15e9), bytes_accessed=int(us * 3.6e6), transcendentals=0
    )


def dot(a, b):
    return jnp.dot(a, b, preferred_element_type=jnp.float32)


def dot_nt(a, b):
    return lax.dot_general(a, b, (((1,), (1,)), ((), ())), preferred_element_type=jnp.float32)


def swap_cp(block, mask):
    count = lax.axis_size("cp")
    return lax.ppermute(block, "cp", [(i, i ^ mask) for i in range(count)])


def shift_cp(block, distance):
    count = lax.axis_size("cp")
    route = [(i, i + distance) for i in range(count) if 0 <= i + distance < count]
    return lax.ppermute(block, "cp", route)


def shift_tp(block, distance):
    count = lax.axis_size("tp")
    return lax.ppermute(block, "tp", [(i, (i + distance) % count) for i in range(count)])


def pool_copies(kv, far, near, keys, values, sems):
    copies = []
    for src, row, rows, place in (
        (kv, 0, ROWS, PRIOR * BLOCK),
        (far, 0, FAR_ROWS, 0),
        (near, 0, ROWS, ROWS - BLOCK),
    ):
        for col, pool in ((0, keys), (HD, values)):
            copies.append(
                pltpu.make_async_copy(
                    src.at[pl.ds(row, rows), pl.ds(col, HD)],
                    pool.at[pl.ds(place, rows)],
                    sems.at[len(copies)],
                )
            )
    return copies


def block_rows(b):
    return pl.ds(pl.multiple_of(b * BLOCK, BLOCK), BLOCK)


def first_mask(odd, width):
    key_pos = lax.broadcasted_iota(jnp.int32, (256, width), 0)
    row_pos = lax.broadcasted_iota(jnp.int32, (256, width), 1) % BLOCK + BLOCK
    return (key_pos <= row_pos) & (key_pos >= odd * BLOCK)


def flipped_heads(block):
    heads = block.shape[1] // HD
    return jnp.concatenate([block[:, h * HD : (h + 1) * HD].T for h in range(heads)], axis=1)


def stacked_heads(block):
    heads = block.shape[1] // HD
    return jnp.concatenate([block[:, h * HD : (h + 1) * HD] for h in range(heads)], axis=0)


def tiles_of(table, b):
    diag = PRIOR + b
    count = diag - jnp.maximum(table[START + b], 0) + 1
    return (count + 1) // 2, count % 2, diag


def low_of(step, odd, diag):
    block = diag - 1 - 2 * step + jnp.where(step > 0, odd, 0)
    return pl.multiple_of(block * BLOCK, BLOCK)


def forward_kernel(
    chunk, table, q_ref, kv, far, near, att, att_t, total_ref, keys, values, sems
):
    copies = pool_copies(kv, far, near, keys, values, sems)
    for copy in copies:
        copy.start()
    for copy in copies:
        copy.wait()

    groups = [slice(at, at + FW) for at in range(0, CW, FW)]

    def block(b, _):
        steps, odd, diag = tiles_of(table, b)
        q_t = [
            flipped_heads(q_ref[block_rows(b), chunk * CW + cols.start : chunk * CW + cols.stop])
            for cols in groups
        ]

        def tile(step, mask, carry):
            low = low_of(step, odd, diag)
            k = keys[pl.ds(low, 256), :]
            v_t = values[pl.ds(low, 256), :].T
            result = []
            for at in range(len(groups)):
                s = dot(k, q_t[at]) * SCALE_LOG2
                if carry is None:
                    s = jnp.where(mask, s, MASKED)
                    top = jnp.max(s, axis=0, keepdims=True)
                    p = jnp.exp2(s - top)
                    total = jnp.sum(p, axis=0, keepdims=True)
                    acc = dot(v_t, p.astype(jnp.bfloat16))
                else:
                    top_old, total, acc = carry[at]
                    top = jnp.maximum(top_old, jnp.max(s, axis=0, keepdims=True))
                    fade = jnp.exp2(top_old - top)
                    p = jnp.exp2(s - top)
                    total = total * fade + jnp.sum(p, axis=0, keepdims=True)
                    acc = acc * fade + dot(v_t, p.astype(jnp.bfloat16))
                result.append((top, total, acc))
            return result

        carry = tile(0, first_mask(odd, FW), None)
        carry = lax.fori_loop(1, steps, lambda step, carry: tile(step, None, carry), carry)
        for cols, (top, total, acc) in zip(groups, carry):
            out = (acc * (1.0 / total)).astype(jnp.bfloat16)
            att_t[b, :, cols] = out
            for head in range(FW // HD):
                at = cols.start + head * HD
                att[block_rows(b), at : at + HD] = out[:, head * HD : (head + 1) * HD].T
            total_ref[b, :, cols] = top + jnp.log2(total)
        return _

    lax.fori_loop(0, BLK_DEV, block, 0)


def forward(table, queries, kv, far, near, chunk):
    def kernel(*refs):
        forward_kernel(chunk, *refs)

    return pl.pallas_call(
        kernel,
        in_specs=[SMEM, WHOLE] + [ANY] * 3,
        out_specs=[WHOLE] * 3,
        out_shape=[
            jax.ShapeDtypeStruct((ROWS, CW), jnp.bfloat16),
            jax.ShapeDtypeStruct((BLK_DEV, HD, CW), jnp.bfloat16),
            jax.ShapeDtypeStruct((BLK_DEV, 1, CW), jnp.float32),
        ],
        scratch_shapes=[
            pltpu.VMEM((POOL * BLOCK, HD), jnp.bfloat16),
            pltpu.VMEM((POOL * BLOCK, HD), jnp.bfloat16),
            pltpu.SemaphoreType.DMA((6,)),
        ],
        compiler_params=PARAMS,
        cost_estimate=lasting(8),
        name="attention_forward",
    )(table, queries, kv, far, near)


def start_chosen(rel, index, sources, place, sem, col=0):
    for at, source in enumerate(sources):
        @pl.when(rel == at)
        def _():
            pltpu.make_async_copy(
                source.at[pl.ds(pl.multiple_of(index * BLOCK, BLOCK), BLOCK)], place, sem
            ).start()


def backward_kernel(chunk, last, first, *refs):
    refs = list(refs)
    table, q_ref, att_t, total_ref, kv, far, near = refs[:7]
    sources = refs[7:11]
    refs = refs[11:]
    if not first:
        key_in, value_in = refs[1:3]
        refs = refs[3:]
    dq_hbm = refs[0]
    if last:
        own_ref, near_ref, far_ref = refs[1:4]
        refs = refs[4:]
        key_acc, value_acc = refs[:2]
    else:
        key_acc, value_acc = refs[1:3]
        refs = refs[3:]
    keys, values, grads, dq, sems, grad_sems, out_sems = refs[-7:]

    incoming = []
    if not first:
        incoming += [
            pltpu.make_async_copy(key_in, key_acc, sems.at[6]),
            pltpu.make_async_copy(value_in, value_acc, sems.at[7]),
        ]
    incoming += pool_copies(kv, far, near, keys, values, sems)
    for at in range(BLK_DEV):
        start_chosen(
            table[GRAD_REL + at], table[GRAD_IDX + at], sources, grads.at[block_rows(at)], grad_sems.at[at]
        )
    for copy in incoming:
        copy.start()
    if first:
        key_acc[...] = jnp.zeros_like(key_acc)
        value_acc[...] = jnp.zeros_like(value_acc)
    for copy in incoming:
        copy.wait()
    for at in range(BLK_DEV):
        pltpu.make_async_copy(
            sources[0].at[pl.ds(0, BLOCK)], grads.at[block_rows(at)], grad_sems.at[at]
        ).wait()

    def outward(b):
        return pltpu.make_async_copy(
            dq.at[block_rows(b)], dq_hbm.at[block_rows(b), pl.ds(chunk * CW, CW)], out_sems.at[b]
        )

    groups = [slice(at, at + BW) for at in range(0, CW, BW)]

    def block(b, _):
        steps, odd, diag = tiles_of(table, b)
        held = []
        for cols in groups:
            q = q_ref[block_rows(b), chunk * CW + cols.start : chunk * CW + cols.stop]
            g = grads[block_rows(b), cols]
            g_t = flipped_heads(g)
            delta = jnp.sum(
                g_t.astype(jnp.float32) * att_t[b, :, cols].astype(jnp.float32),
                axis=0,
                keepdims=True,
            )
            held.append(
                (flipped_heads(q), stacked_heads(q), g_t, stacked_heads(g), delta, total_ref[b, :, cols])
            )

        def tile(step, mask, carry):
            low = low_of(step, odd, diag)
            k = keys[pl.ds(low, 256), :]
            k_t = k.T
            v = values[pl.ds(low, 256), :]
            result = []
            key_part = value_part = None
            for at, (q_t, q_s, g_t, g_s, delta, log_total) in enumerate(held):
                s = dot(k, q_t) * SCALE_LOG2
                if mask is not None:
                    s = jnp.where(mask, s, MASKED)
                p = jnp.exp2(s - log_total).astype(jnp.bfloat16)
                dp = dot(v, g_t)
                ds = (p.astype(jnp.float32) * (dp - delta)).astype(jnp.bfloat16)
                value_term, key_term, query_term = dot(p, g_s), dot(ds, q_s), dot(k_t, ds)
                value_part = value_term if value_part is None else value_part + value_term
                key_part = key_term if key_part is None else key_part + key_term
                result.append(query_term if carry is None else carry[at] + query_term)
            value_acc[pl.ds(low, 256), :] += value_part
            key_acc[pl.ds(low, 256), :] += key_part
            return result

        carry = tile(0, first_mask(odd, BW), None)
        carry = lax.fori_loop(1, steps, lambda step, carry: tile(step, None, carry), carry)
        for cols, dq_t in zip(groups, carry):
            dq_t = (dq_t * SCALE).astype(jnp.bfloat16)
            for head in range(BW // HD):
                at = cols.start + head * HD
                dq[block_rows(b), at : at + HD] = dq_t[:, head * HD : (head + 1) * HD].T
        outward(b).start()
        return _

    lax.fori_loop(0, BLK_DEV, block, 0)

    if last:
        near_at = ROWS - BLOCK
        own_at = PRIOR * BLOCK
        for acc, cols, factor in ((key_acc, slice(0, HD), SCALE), (value_acc, slice(HD, 2 * HD), 1.0)):
            own_ref[:, cols] = acc[own_at:] * factor
            near_ref[:, cols] = (acc[near_at:own_at] * factor).astype(jnp.bfloat16)
            far_ref[:, cols] = (acc[:near_at] * factor).astype(jnp.bfloat16)
    for b in range(BLK_DEV):
        outward(b).wait()


def backward(table, queries, att_t, totals, pool, sources, carried, chunk, last):
    first = carried is None
    pool_shape = (POOL * BLOCK, HD)
    sums = [jax.ShapeDtypeStruct(pool_shape, jnp.float32)] * 2
    if last:
        out_shape = [
            jax.ShapeDtypeStruct((ROWS, 2 * HD), jnp.float32),
            jax.ShapeDtypeStruct((ROWS, 2 * HD), jnp.bfloat16),
            jax.ShapeDtypeStruct((FAR_ROWS, 2 * HD), jnp.bfloat16),
        ]
        scratch = [pltpu.VMEM(pool_shape, jnp.float32)] * 2
    else:
        out_shape, scratch = sums, []

    def kernel(*refs):
        backward_kernel(chunk, last, first, *refs)

    return pl.pallas_call(
        kernel,
        in_specs=[SMEM] + [WHOLE] * 3 + [ANY] * (7 if first else 10),
        out_specs=[ANY] + [WHOLE] * len(out_shape),
        out_shape=[jax.ShapeDtypeStruct((ROWS, WIDTH), jnp.bfloat16)] + out_shape,
        input_output_aliases={} if first else {11: 0},
        scratch_shapes=scratch
        + [
            pltpu.VMEM(pool_shape, jnp.bfloat16),
            pltpu.VMEM(pool_shape, jnp.bfloat16),
            pltpu.VMEM((ROWS, CW), jnp.bfloat16),
            pltpu.VMEM((ROWS, CW), jnp.bfloat16),
            pltpu.SemaphoreType.DMA((8,)),
            pltpu.SemaphoreType.DMA((BLK_DEV,)),
            pltpu.SemaphoreType.DMA((BLK_DEV,)),
        ],
        compiler_params=PARAMS,
        cost_estimate=lasting(9),
        name="attention_backward",
    )(table, queries, att_t, totals, *pool, *sources, *([] if first else carried))


def grad_matmul_kernel(
    table, own, ahead_rows, opposite_upper, opposite_lower, before_rows, weight_hbm, *refs
):
    outs, weight, sems = refs[:CHUNKS], *refs[CHUNKS:]
    half = ROWS // 2
    copies = []
    for chunk in range(CHUNKS):
        for ahead in range(4):
            at = pl.multiple_of(((table[TP] + ahead) % 4) * WIDTH, WIDTH)
            copies.append(
                pltpu.make_async_copy(
                    weight_hbm.at[pl.ds(chunk * CW, CW), pl.ds(at, WIDTH)],
                    weight.at[4 * chunk + ahead],
                    sems.at[4 * chunk + ahead],
                )
            )
            copies[-1].start()
    for chunk in range(CHUNKS):
        total = None
        for ahead, rows in enumerate((own, ahead_rows, None, before_rows)):
            slot = 4 * chunk + ahead
            copies[slot].wait()
            if rows is None:
                term = jnp.concatenate(
                    [
                        dot_nt(part[...], weight[slot]) for part in (opposite_upper, opposite_lower)
                    ],
                    axis=0,
                )
            else:
                term = dot_nt(rows[...], weight[slot])
            total = term if total is None else total + term
        outs[chunk][...] = total.astype(jnp.bfloat16)


def grad_matmul(table, pieces, weight):
    return pl.pallas_call(
        grad_matmul_kernel,
        in_specs=[SMEM] + [WHOLE] * 5 + [ANY],
        out_specs=[WHOLE] * CHUNKS,
        out_shape=[jax.ShapeDtypeStruct((ROWS, CW), jnp.bfloat16)] * CHUNKS,
        scratch_shapes=[
            pltpu.VMEM((4 * CHUNKS, CW, WIDTH), jnp.bfloat16),
            pltpu.SemaphoreType.DMA((4 * CHUNKS,)),
        ],
        compiler_params=PARAMS,
        cost_estimate=lasting(7),
        name="grad_projection",
    )(table, *pieces, weight)


HALF = WIDTH // 2


def weight_copy(table, weight_hbm, weight, slot, ahead, half, sem):
    at = pl.multiple_of(((table[TP] + ahead) % 4) * WIDTH + half * HALF, HALF)
    return pltpu.make_async_copy(weight_hbm.at[:, pl.ds(at, HALF)], weight.at[slot], sem)


def product_kernel(table, *refs):
    sources = [refs[4 * c : 4 * c + 4] for c in range(CHUNKS)]
    weight_hbm, left, right, onward, back, own, rows, weight, sems, weight_sems = refs[4 * CHUNKS :]

    def place(c, at):
        return rows.at[block_rows(at), pl.ds(c * CW, CW)]

    places = [(c, at, c * BLK_DEV + at) for c in range(CHUNKS) for at in range(BLK_DEV)]
    for c, at, sem in places:
        start_chosen(
            table[ATT_REL + at], table[ATT_IDX + at], sources[c], place(c, at), sems.at[sem]
        )
    parts = ((2, 0), (2, 1), (1, 1), (3, 0), (0, 0), (0, 1))
    weights = [
        weight_copy(table, weight_hbm, weight, slot, ahead, half, weight_sems.at[slot])
        for slot, (ahead, half) in enumerate(parts)
    ]
    for copy in weights:
        copy.start()
    for c, at, sem in places:
        pltpu.make_async_copy(sources[c][0].at[pl.ds(0, BLOCK)], place(c, at), sems.at[sem]).wait()
    for slot, out in enumerate((left, right, onward, back)):
        weights[slot].wait()
        out[...] = dot(rows[...], weight[slot]).astype(jnp.bfloat16)
    for slot in (4, 5):
        weights[slot].wait()
        own[:, (slot - 4) * HALF : (slot - 3) * HALF] = dot(rows[...], weight[slot]).astype(
            jnp.bfloat16
        )


def products(table, sources, weight):
    flat = [source for group in sources for source in group]
    return pl.pallas_call(
        product_kernel,
        in_specs=[SMEM] + [ANY] * (4 * CHUNKS + 1),
        out_specs=[WHOLE] * 6,
        out_shape=[jax.ShapeDtypeStruct((ROWS, HALF), jnp.bfloat16)] * 4
        + [jax.ShapeDtypeStruct((ROWS, WIDTH), jnp.bfloat16)] * 2,
        scratch_shapes=[
            pltpu.VMEM((6, WIDTH, HALF), jnp.bfloat16),
            pltpu.SemaphoreType.DMA((4 * CHUNKS,)),
            pltpu.SemaphoreType.DMA((6,)),
        ],
        compiler_params=PARAMS,
        cost_estimate=lasting(7),
        name="products",
    )(table, *flat, weight)


def sum_product_kernel(table, rows, weight_hbm, before, after_, onward, back, weight, sems):
    weights = [
        weight_copy(table, weight_hbm, weight, 0, 1, 0, sems.at[0]),
        weight_copy(table, weight_hbm, weight, 1, 3, 1, sems.at[1]),
    ]
    for copy in weights:
        copy.start()
    for slot, (extra, out) in enumerate(((before, onward), (after_, back))):
        weights[slot].wait()
        value = dot(rows[...], weight[slot])
        out[...] = (value + extra[...].astype(jnp.float32)).astype(jnp.bfloat16)


def sum_products(table, rows, weight, before, after):
    half = jax.ShapeDtypeStruct((ROWS, HALF), jnp.bfloat16)
    return pl.pallas_call(
        sum_product_kernel,
        in_specs=[SMEM, WHOLE, ANY, WHOLE, WHOLE],
        out_specs=[WHOLE] * 2,
        out_shape=[half] * 2,
        scratch_shapes=[
            pltpu.VMEM((2, WIDTH, HALF), jnp.bfloat16),
            pltpu.SemaphoreType.DMA((2,)),
        ],
        compiler_params=PARAMS,
        cost_estimate=lasting(4),
        name="sum_products",
    )(table, rows, weight, before, after)


def last_sum_kernel(own, before_a, before_b, after_a, after_b, out):
    for half, before, after in ((0, before_a, after_a), (1, before_b, after_b)):
        cols = slice(half * 512, (half + 1) * 512)
        out[:, cols] = (
            own[:, cols].astype(jnp.float32) + before[...].astype(jnp.float32) + after[...].astype(jnp.float32)
        ).astype(jnp.bfloat16)


def last_sum(own, before_a, before_b, after_a, after_b):
    part = pl.BlockSpec((BLOCK, 512), lambda j: (j, 0))
    full = pl.BlockSpec((BLOCK, WIDTH), lambda j: (j, 0))
    return pl.pallas_call(
        last_sum_kernel,
        grid=(4,),
        in_specs=[full, part, part, part, part],
        out_specs=full,
        out_shape=jax.ShapeDtypeStruct((ROWS, WIDTH), jnp.bfloat16),
        compiler_params=PARAMS,
        cost_estimate=lasting(2),
        name="last_sum",
    )(own, before_a, before_b, after_a, after_b)


def scalar_table(doc_start, balanced_source):
    device = lax.axis_index("cp")
    member = device % GROUP
    group_blocks = GROUP * BLK_DEV
    group_first = device // GROUP * group_blocks
    sources = lax.dynamic_slice_in_dim(balanced_source, group_first, group_blocks) - group_first
    slots = jnp.arange(group_blocks, dtype=jnp.int32)
    slot_of = jnp.sum(
        jnp.where(sources[None, :] == slots[:, None], slots[None, :], 0), axis=1, dtype=jnp.int32
    )
    mine = member * BLK_DEV
    wanted = lax.dynamic_slice_in_dim(sources, mine, BLK_DEV)
    held = lax.dynamic_slice_in_dim(slot_of, mine, BLK_DEV)
    starts = lax.dynamic_slice_in_dim(doc_start, device * BLK_DEV, BLK_DEV)
    starts = starts - (device * BLK_DEV - PRIOR)
    return jnp.concatenate(
        [
            starts,
            (held // BLK_DEV) ^ member,
            held % BLK_DEV,
            (wanted // BLK_DEV) ^ member,
            wanted % BLK_DEV,
            jnp.stack([device % 2, lax.axis_index("tp")]),
        ]
    ).astype(jnp.int32)


def group_exchange(block, earlier):
    across = swap_cp(block, 2)
    return [block, swap_cp(after(block, earlier), 1), across, swap_cp(after(across, earlier), 1)]


def copy_all(*pairs, sems):
    copies = [pltpu.make_async_copy(src, dst, sems.at[at]) for at, (src, dst) in enumerate(pairs)]
    for copy in copies:
        copy.start()
    for copy in copies:
        copy.wait()


def join_kernel(keys, values, kv, last, sems):
    tail = pl.ds(ROWS - FAR_ROWS, FAR_ROWS)
    left, right = pl.ds(0, HD), pl.ds(HD, HD)
    copy_all(
        (keys, kv.at[:, left]),
        (values, kv.at[:, right]),
        (keys.at[tail], last.at[:, left]),
        (values.at[tail], last.at[:, right]),
        sems=sems,
    )


def join(keys, values):
    return pl.pallas_call(
        join_kernel,
        in_specs=[HBM] * 2,
        out_specs=[WHOLE] * 2,
        out_shape=[
            jax.ShapeDtypeStruct((ROWS, 2 * HD), jnp.bfloat16),
            jax.ShapeDtypeStruct((FAR_ROWS, 2 * HD), jnp.bfloat16),
        ],
        scratch_shapes=[pltpu.SemaphoreType.DMA((4,))],
        compiler_params=PARAMS,
        cost_estimate=lasting(2),
        name="join",
    )(keys, values)


def halve_kernel(before, ahead, upper, lower, sems):
    half = ROWS // 2
    copy_all((before.at[pl.ds(0, half)], upper), (ahead.at[pl.ds(half, half)], lower), sems=sems)


def halve(before, ahead):
    return pl.pallas_call(
        halve_kernel,
        in_specs=[ANY] * 2,
        out_specs=[WHOLE] * 2,
        out_shape=[jax.ShapeDtypeStruct((ROWS // 2, WIDTH), jnp.bfloat16)] * 2,
        scratch_shapes=[pltpu.SemaphoreType.DMA((2,))],
        compiler_params=PARAMS,
        cost_estimate=lasting(1),
        name="halve",
    )(before, ahead)


def add_kernel(own, near, far, keys, values):
    total = own[...] + near[...].astype(jnp.float32)
    front = total[: ROWS - FAR_ROWS].astype(jnp.bfloat16)
    rear = (total[ROWS - FAR_ROWS :] + far[...].astype(jnp.float32)).astype(jnp.bfloat16)
    for col, out in ((0, keys), (HD, values)):
        out[: ROWS - FAR_ROWS] = front[:, col : col + HD]
        out[ROWS - FAR_ROWS :] = rear[:, col : col + HD]


def add_terms(own, near, far):
    return pl.pallas_call(
        add_kernel,
        in_specs=[WHOLE] * 3,
        out_specs=[WHOLE] * 2,
        out_shape=[jax.ShapeDtypeStruct((ROWS, HD), jnp.bfloat16)] * 2,
        compiler_params=PARAMS,
        cost_estimate=lasting(1),
        name="add_terms",
    )(own, near, far)


def after(value, earlier):
    return lax.optimization_barrier((value, earlier))[0]


def shards(queries, key_rows, value_rows, out_proj, grad_mixed, doc_start, balanced_source):
    table = scalar_table(doc_start, balanced_source)

    kv, last = join(key_rows, value_rows)
    far = shift_cp(last, 2)
    near = shift_cp(kv, 1)
    pool = (kv, far, near)

    grads_in = after(grad_mixed, kv)
    grads_before = shift_tp(grads_in, 1)
    grads_ahead = shift_tp(grads_in, -1)

    attended, attended_t, totals = [], [], []
    for chunk in range(CHUNKS):
        att, att_t, total = forward(
            after(table, (attended[0], upper, lower))
            if chunk
            else table,
            queries,
            *pool,
            chunk,
        )
        if chunk == 0:
            upper, lower = halve(after(grads_before, att), grads_ahead)
        attended.append(att)
        attended_t.append(att_t)
        totals.append(total)

    pieces = (grad_mixed, grads_ahead, shift_tp(upper, 1), shift_tp(lower, -1), grads_before)
    exchanged = [group_exchange(attended[0], attended[1]), None]
    grad_attended = grad_matmul(table, pieces, out_proj)
    exchanged[1] = group_exchange(attended[1], grad_attended[1])
    grad_across = swap_cp(grad_attended[0], 2)

    far_left, far_right, onward_b, back_a, own, rows = products(
        after(table, grad_attended[1]), exchanged, out_proj
    )
    from_before = shift_tp(far_left, 1)
    from_after = shift_tp(far_right, -1)

    grad_sources = [
        [
            grad_attended[0],
            swap_cp(after(grad_attended[0], own), 1),
            grad_across,
            swap_cp(after(grad_across, own), 1),
        ]
    ]
    carried = backward(
        after(table, own),
        queries, attended_t[0], totals[0], pool, grad_sources[0], None, 0, False,
    )
    query_a = carried[1]
    across = swap_cp(after(grad_attended[1], tuple(grad_sources[0])), 2)
    grad_sources.append(
        [
            grad_attended[1],
            swap_cp(after(grad_attended[1], query_a), 1),
            across,
            swap_cp(after(across, query_a), 1),
        ]
    )
    before_b = shift_tp(onward_b, 1)
    after_a = shift_tp(back_a, -1)
    onward_a, back_b = sum_products(after(table, query_a), rows, out_proj, from_before, from_after)
    before_a = shift_tp(onward_a, 1)
    after_b = shift_tp(back_b, -1)
    query_grad, own_grads, near_grads, far_grads = backward(
        after(table, (onward_a, before_b, after_a)),
        queries, attended_t[1], totals[1], pool, grad_sources[1], carried, 1, True,
    )
    far_back = shift_cp(after(far_grads, (before_b, after_a)), -2)
    near_back = shift_cp(after(near_grads, (before_b, after_a)), -1)
    mixed = last_sum(own, before_a, before_b, after_a, after_b)
    key_grad, value_grad = add_terms(after(own_grads, mixed), near_back, far_back)
    return (mixed, query_grad, key_grad, value_grad)


def solution(mesh):
    placed = (P("cp", "tp"), P("cp", "tp"), P("cp", "tp"), P("tp", None), P("cp", "tp"), P(), P())
    return jax.shard_map(
        shards,
        mesh=mesh,
        in_specs=placed,
        out_specs=(P("cp", "tp"),) * 4,
        check_vma=False,
    )
```

```python
import math

import jax
import jax.numpy as jnp
from jax import lax
from jax.experimental import pallas as pl
from jax.experimental.pallas import tpu as pltpu
from jax.sharding import PartitionSpec as P

HD = 128
BLOCK = 128
BLK_DEV = 4
MAXB = 8
GROUP = 4
PRIOR = MAXB - 1
POOL = PRIOR + BLK_DEV
ROWS = BLOCK * BLK_DEV
WIDTH = 1024
FAR_ROWS = (PRIOR - BLK_DEV) * BLOCK
CHUNKS = 2
CW = WIDTH // CHUNKS
FW = 512
BW = 512

SCALE = 1.0 / math.sqrt(HD)
SCALE_LOG2 = SCALE * math.log2(math.e)
MASKED = -1e30

START, GRAD_REL, GRAD_IDX, ATT_REL, ATT_IDX, CORE, TP = 0, 4, 8, 12, 16, 20, 21

ANY = pl.BlockSpec(memory_space=pl.ANY)
WHOLE = pl.BlockSpec(memory_space=pltpu.VMEM)
HBM = pl.BlockSpec(memory_space=pltpu.HBM)
SMEM = pl.BlockSpec(memory_space=pltpu.SMEM)
VMEM_LIMIT = 48 * 1024 * 1024


PARAMS = pltpu.CompilerParams(vmem_limit_bytes=VMEM_LIMIT)


def lasting(us):
    return pl.CostEstimate(
        flops=int(us * 1.15e9), bytes_accessed=int(us * 3.6e6), transcendentals=0
    )


def dot(a, b):
    return jnp.dot(a, b, preferred_element_type=jnp.float32)


def dot_nt(a, b):
    return lax.dot_general(a, b, (((1,), (1,)), ((), ())), preferred_element_type=jnp.float32)


def swap_cp(block, mask):
    count = lax.axis_size("cp")
    return lax.ppermute(block, "cp", [(i, i ^ mask) for i in range(count)])


def shift_cp(block, distance):
    count = lax.axis_size("cp")
    route = [(i, i + distance) for i in range(count) if 0 <= i + distance < count]
    return lax.ppermute(block, "cp", route)


def shift_tp(block, distance):
    count = lax.axis_size("tp")
    return lax.ppermute(block, "tp", [(i, (i + distance) % count) for i in range(count)])


def pool_copies(kv, far, near, keys, values, sems):
    copies = []
    for src, row, rows, place in (
        (kv, 0, ROWS, PRIOR * BLOCK),
        (far, 0, FAR_ROWS, 0),
        (near, 0, ROWS, ROWS - BLOCK),
    ):
        for col, pool in ((0, keys), (HD, values)):
            copies.append(
                pltpu.make_async_copy(
                    src.at[pl.ds(row, rows), pl.ds(col, HD)],
                    pool.at[pl.ds(place, rows)],
                    sems.at[len(copies)],
                )
            )
    return copies


def block_rows(b):
    return pl.ds(pl.multiple_of(b * BLOCK, BLOCK), BLOCK)


def first_mask(odd, width):
    key_pos = lax.broadcasted_iota(jnp.int32, (256, width), 0)
    row_pos = lax.broadcasted_iota(jnp.int32, (256, width), 1) % BLOCK + BLOCK
    return (key_pos <= row_pos) & (key_pos >= odd * BLOCK)


def flipped_heads(block):
    heads = block.shape[1] // HD
    return jnp.concatenate([block[:, h * HD : (h + 1) * HD].T for h in range(heads)], axis=1)


def stacked_heads(block):
    heads = block.shape[1] // HD
    return jnp.concatenate([block[:, h * HD : (h + 1) * HD] for h in range(heads)], axis=0)


def tiles_of(table, b):
    diag = PRIOR + b
    count = diag - jnp.maximum(table[START + b], 0) + 1
    return (count + 1) // 2, count % 2, diag


def low_of(step, odd, diag):
    block = diag - 1 - 2 * step + jnp.where(step > 0, odd, 0)
    return pl.multiple_of(block * BLOCK, BLOCK)


def forward_kernel(
    chunk, table, q_ref, *refs
):
    if chunk == 0:
        kv, far, near, att, att_t, total_ref, keys, values, sems = refs
        copies = pool_copies(kv, far, near, keys, values, sems)
        for copy in copies:
            copy.start()
        for copy in copies:
            copy.wait()
    else:
        keys, values, att, att_t, total_ref = refs

    groups = [slice(at, at + FW) for at in range(0, CW, FW)]

    def block(b, _):
        steps, odd, diag = tiles_of(table, b)
        q_t = [
            flipped_heads(q_ref[block_rows(b), chunk * CW + cols.start : chunk * CW + cols.stop])
            for cols in groups
        ]

        def tile(step, mask, carry):
            low = low_of(step, odd, diag)
            k = keys[pl.ds(low, 256), :]
            v_t = values[pl.ds(low, 256), :].T
            result = []
            for at in range(len(groups)):
                s = dot(k, q_t[at]) * SCALE_LOG2
                if carry is None:
                    s = jnp.where(mask, s, MASKED)
                    top = jnp.max(s, axis=0, keepdims=True)
                    p = jnp.exp2(s - top)
                    total = jnp.sum(p, axis=0, keepdims=True)
                    acc = dot(v_t, p.astype(jnp.bfloat16))
                else:
                    top_old, total, acc = carry[at]
                    top = jnp.maximum(top_old, jnp.max(s, axis=0, keepdims=True))
                    fade = jnp.exp2(top_old - top)
                    p = jnp.exp2(s - top)
                    total = total * fade + jnp.sum(p, axis=0, keepdims=True)
                    acc = acc * fade + dot(v_t, p.astype(jnp.bfloat16))
                result.append((top, total, acc))
            return result

        carry = tile(0, first_mask(odd, FW), None)
        carry = lax.fori_loop(1, steps, lambda step, carry: tile(step, None, carry), carry)
        for cols, (top, total, acc) in zip(groups, carry):
            out = (acc * (1.0 / total)).astype(jnp.bfloat16)
            att_t[b, :, cols] = out
            for head in range(FW // HD):
                at = cols.start + head * HD
                att[block_rows(b), at : at + HD] = out[:, head * HD : (head + 1) * HD].T
            total_ref[b, :, cols] = top + jnp.log2(total)
        return _

    lax.fori_loop(0, BLK_DEV, block, 0)


def forward(table, queries, pool, chunk):
    first = chunk == 0
    pool_shape = jax.ShapeDtypeStruct((POOL * BLOCK, HD), jnp.bfloat16)

    def kernel(*refs):
        forward_kernel(chunk, *refs)

    return pl.pallas_call(
        kernel,
        in_specs=[SMEM, WHOLE] + ([ANY] * 3 if first else [WHOLE] * 2),
        out_specs=[WHOLE] * (5 if first else 3),
        out_shape=[
            jax.ShapeDtypeStruct((ROWS, CW), jnp.bfloat16),
            jax.ShapeDtypeStruct((BLK_DEV, HD, CW), jnp.bfloat16),
            jax.ShapeDtypeStruct((BLK_DEV, 1, CW), jnp.float32),
        ]
        + ([pool_shape] * 2 if first else []),
        scratch_shapes=[pltpu.SemaphoreType.DMA((6,))] if first else [],
        compiler_params=PARAMS,
        cost_estimate=lasting(8),
        name="attention_forward",
    )(table, queries, *pool)


def start_chosen(rel, index, sources, place, sem, col=0):
    for at, source in enumerate(sources):
        @pl.when(rel == at)
        def _():
            pltpu.make_async_copy(
                source.at[pl.ds(pl.multiple_of(index * BLOCK, BLOCK), BLOCK)], place, sem
            ).start()


def backward_kernel(chunk, last, first, *refs):
    refs = list(refs)
    table, q_ref, att_t, total_ref, keys, values = refs[:6]
    sources = refs[6:10]
    refs = refs[10:]
    if not first:
        key_in, value_in = refs[1:3]
        refs = refs[3:]
    dq_hbm = refs[0]
    if last:
        own_ref, near_ref, far_ref = refs[1:4]
        refs = refs[4:]
        key_acc, value_acc = refs[:2]
    else:
        key_acc, value_acc = refs[1:3]
        refs = refs[3:]
    grads, dq, grad_sems, out_sems = refs[-4:]

    for at in range(BLK_DEV):
        start_chosen(
            table[GRAD_REL + at], table[GRAD_IDX + at], sources, grads.at[block_rows(at)], grad_sems.at[at]
        )
    key_acc[...] = jnp.zeros_like(key_acc)
    value_acc[...] = jnp.zeros_like(value_acc)
    for at in range(BLK_DEV):
        pltpu.make_async_copy(
            sources[0].at[pl.ds(0, BLOCK)], grads.at[block_rows(at)], grad_sems.at[at]
        ).wait()

    def outward(b):
        return pltpu.make_async_copy(
            dq.at[block_rows(b)], dq_hbm.at[block_rows(b), pl.ds(chunk * CW, CW)], out_sems.at[b]
        )

    groups = [slice(at, at + BW) for at in range(0, CW, BW)]

    def block(b, _):
        steps, odd, diag = tiles_of(table, b)
        held = []
        for cols in groups:
            q = q_ref[block_rows(b), chunk * CW + cols.start : chunk * CW + cols.stop]
            g = grads[block_rows(b), cols]
            g_t = flipped_heads(g)
            delta = jnp.sum(
                g_t.astype(jnp.float32) * att_t[b, :, cols].astype(jnp.float32),
                axis=0,
                keepdims=True,
            )
            held.append(
                (flipped_heads(q), stacked_heads(q), g_t, stacked_heads(g), delta, total_ref[b, :, cols])
            )

        def tile(step, mask, carry):
            low = low_of(step, odd, diag)
            k = keys[pl.ds(low, 256), :]
            k_t = k.T
            v = values[pl.ds(low, 256), :]
            result = []
            key_part = value_part = None
            for at, (q_t, q_s, g_t, g_s, delta, log_total) in enumerate(held):
                s = dot(k, q_t) * SCALE_LOG2
                if mask is not None:
                    s = jnp.where(mask, s, MASKED)
                p = jnp.exp2(s - log_total).astype(jnp.bfloat16)
                dp = dot(v, g_t)
                ds = (p.astype(jnp.float32) * (dp - delta)).astype(jnp.bfloat16)
                value_term, key_term, query_term = dot(p, g_s), dot(ds, q_s), dot(k_t, ds)
                value_part = value_term if value_part is None else value_part + value_term
                key_part = key_term if key_part is None else key_part + key_term
                result.append(query_term if carry is None else carry[at] + query_term)
            value_acc[pl.ds(low, 256), :] += value_part
            key_acc[pl.ds(low, 256), :] += key_part
            return result

        carry = tile(0, first_mask(odd, BW), None)
        carry = lax.fori_loop(1, steps, lambda step, carry: tile(step, None, carry), carry)
        for cols, dq_t in zip(groups, carry):
            dq_t = (dq_t * SCALE).astype(jnp.bfloat16)
            for head in range(BW // HD):
                at = cols.start + head * HD
                dq[block_rows(b), at : at + HD] = dq_t[:, head * HD : (head + 1) * HD].T
        outward(b).start()
        return _

    lax.fori_loop(0, BLK_DEV, block, 0)

    if last:
        near_at = ROWS - BLOCK
        own_at = PRIOR * BLOCK
        for acc, earlier, cols, factor in (
            (key_acc, key_in, slice(0, HD), SCALE),
            (value_acc, value_in, slice(HD, 2 * HD), 1.0),
        ):
            def total(rows):
                return (acc[rows] + earlier[rows]) * factor

            far_ref[:, cols] = total(slice(0, near_at)).astype(jnp.bfloat16)
            near_ref[:, cols] = total(slice(near_at, own_at)).astype(jnp.bfloat16)
            own_ref[:, cols] = total(slice(own_at, None))
    for b in range(BLK_DEV):
        outward(b).wait()


def backward(table, queries, att_t, totals, pool, sources, carried, chunk, last):
    first = carried is None
    pool_shape = (POOL * BLOCK, HD)
    sums = [jax.ShapeDtypeStruct(pool_shape, jnp.float32)] * 2
    if last:
        out_shape = [
            jax.ShapeDtypeStruct((ROWS, 2 * HD), jnp.float32),
            jax.ShapeDtypeStruct((ROWS, 2 * HD), jnp.bfloat16),
            jax.ShapeDtypeStruct((FAR_ROWS, 2 * HD), jnp.bfloat16),
        ]
        scratch = [pltpu.VMEM(pool_shape, jnp.float32)] * 2
    else:
        out_shape, scratch = sums, []

    def kernel(*refs):
        backward_kernel(chunk, last, first, *refs)

    return pl.pallas_call(
        kernel,
        in_specs=[SMEM] + [WHOLE] * 5 + [ANY] * 4 + ([] if first else [ANY, WHOLE, WHOLE]),
        out_specs=[ANY] + [WHOLE] * len(out_shape),
        out_shape=[jax.ShapeDtypeStruct((ROWS, WIDTH), jnp.bfloat16)] + out_shape,
        input_output_aliases={} if first else {10: 0},
        scratch_shapes=scratch
        + [
            pltpu.VMEM((ROWS, CW), jnp.bfloat16),
            pltpu.VMEM((ROWS, CW), jnp.bfloat16),
            pltpu.SemaphoreType.DMA((BLK_DEV,)),
            pltpu.SemaphoreType.DMA((BLK_DEV,)),
        ],
        compiler_params=PARAMS,
        cost_estimate=lasting(9),
        name="attention_backward",
    )(table, queries, att_t, totals, *pool, *sources, *([] if first else carried))


def grad_matmul_kernel(
    table, own, ahead_rows, opposite_upper, opposite_lower, before_rows, weight_hbm, *refs
):
    outs, weight, sems = refs[:CHUNKS], *refs[CHUNKS:]
    half = ROWS // 2
    copies = []
    for chunk in range(CHUNKS):
        for ahead in range(4):
            at = pl.multiple_of(((table[TP] + ahead) % 4) * WIDTH, WIDTH)
            copies.append(
                pltpu.make_async_copy(
                    weight_hbm.at[pl.ds(chunk * CW, CW), pl.ds(at, WIDTH)],
                    weight.at[4 * chunk + ahead],
                    sems.at[4 * chunk + ahead],
                )
            )
            copies[-1].start()
    for chunk in range(CHUNKS):
        total = None
        for ahead, rows in enumerate((own, ahead_rows, None, before_rows)):
            slot = 4 * chunk + ahead
            copies[slot].wait()
            if rows is None:
                term = jnp.concatenate(
                    [
                        dot_nt(part[...], weight[slot]) for part in (opposite_upper, opposite_lower)
                    ],
                    axis=0,
                )
            else:
                term = dot_nt(rows[...], weight[slot])
            total = term if total is None else total + term
        outs[chunk][...] = total.astype(jnp.bfloat16)


def grad_matmul(table, pieces, weight):
    return pl.pallas_call(
        grad_matmul_kernel,
        in_specs=[SMEM] + [WHOLE] * 5 + [ANY],
        out_specs=[WHOLE] * CHUNKS,
        out_shape=[jax.ShapeDtypeStruct((ROWS, CW), jnp.bfloat16)] * CHUNKS,
        scratch_shapes=[
            pltpu.VMEM((4 * CHUNKS, CW, WIDTH), jnp.bfloat16),
            pltpu.SemaphoreType.DMA((4 * CHUNKS,)),
        ],
        compiler_params=PARAMS,
        cost_estimate=lasting(7),
        name="grad_projection",
    )(table, *pieces, weight)


HALF = WIDTH // 2


def weight_copy(table, weight_hbm, weight, slot, ahead, half, sem):
    at = pl.multiple_of(((table[TP] + ahead) % 4) * WIDTH + half * HALF, HALF)
    return pltpu.make_async_copy(weight_hbm.at[:, pl.ds(at, HALF)], weight.at[slot], sem)


def product_kernel(table, *refs):
    sources = [refs[4 * c : 4 * c + 4] for c in range(CHUNKS)]
    weight_hbm, left, right, onward, back, own, rows, weight, sems, weight_sems = refs[4 * CHUNKS :]

    def place(c, at):
        return rows.at[block_rows(at), pl.ds(c * CW, CW)]

    places = [(c, at, c * BLK_DEV + at) for c in range(CHUNKS) for at in range(BLK_DEV)]
    for c, at, sem in places:
        start_chosen(
            table[ATT_REL + at], table[ATT_IDX + at], sources[c], place(c, at), sems.at[sem]
        )
    parts = ((2, 0), (2, 1), (1, 1), (3, 0), (0, 0), (0, 1))
    weights = [
        weight_copy(table, weight_hbm, weight, slot, ahead, half, weight_sems.at[slot])
        for slot, (ahead, half) in enumerate(parts)
    ]
    for copy in weights:
        copy.start()
    for c, at, sem in places:
        pltpu.make_async_copy(sources[c][0].at[pl.ds(0, BLOCK)], place(c, at), sems.at[sem]).wait()
    for slot, out in enumerate((left, right, onward, back)):
        weights[slot].wait()
        out[...] = dot(rows[...], weight[slot]).astype(jnp.bfloat16)
    for slot in (4, 5):
        weights[slot].wait()
        own[:, (slot - 4) * HALF : (slot - 3) * HALF] = dot(rows[...], weight[slot]).astype(
            jnp.bfloat16
        )


def products(table, sources, weight):
    flat = [source for group in sources for source in group]
    return pl.pallas_call(
        product_kernel,
        in_specs=[SMEM] + [ANY] * (4 * CHUNKS + 1),
        out_specs=[WHOLE] * 6,
        out_shape=[jax.ShapeDtypeStruct((ROWS, HALF), jnp.bfloat16)] * 4
        + [jax.ShapeDtypeStruct((ROWS, WIDTH), jnp.bfloat16)] * 2,
        scratch_shapes=[
            pltpu.VMEM((6, WIDTH, HALF), jnp.bfloat16),
            pltpu.SemaphoreType.DMA((4 * CHUNKS,)),
            pltpu.SemaphoreType.DMA((6,)),
        ],
        compiler_params=PARAMS,
        cost_estimate=lasting(7),
        name="products",
    )(table, *flat, weight)


def sum_product_kernel(table, rows, weight_hbm, before, after_, onward, back, weight, sems):
    weights = [
        weight_copy(table, weight_hbm, weight, 0, 1, 0, sems.at[0]),
        weight_copy(table, weight_hbm, weight, 1, 3, 1, sems.at[1]),
    ]
    for copy in weights:
        copy.start()
    for slot, (extra, out) in enumerate(((before, onward), (after_, back))):
        weights[slot].wait()
        value = dot(rows[...], weight[slot])
        out[...] = (value + extra[...].astype(jnp.float32)).astype(jnp.bfloat16)


def sum_products(table, rows, weight, before, after):
    half = jax.ShapeDtypeStruct((ROWS, HALF), jnp.bfloat16)
    return pl.pallas_call(
        sum_product_kernel,
        in_specs=[SMEM, WHOLE, ANY, WHOLE, WHOLE],
        out_specs=[WHOLE] * 2,
        out_shape=[half] * 2,
        scratch_shapes=[
            pltpu.VMEM((2, WIDTH, HALF), jnp.bfloat16),
            pltpu.SemaphoreType.DMA((2,)),
        ],
        compiler_params=PARAMS,
        cost_estimate=lasting(4),
        name="sum_products",
    )(table, rows, weight, before, after)


def last_sum_kernel(own, before_a, before_b, after_a, after_b, out):
    for half, before, after in ((0, before_a, after_a), (1, before_b, after_b)):
        cols = slice(half * 512, (half + 1) * 512)
        out[:, cols] = (
            own[:, cols].astype(jnp.float32) + before[...].astype(jnp.float32) + after[...].astype(jnp.float32)
        ).astype(jnp.bfloat16)


def last_sum(own, before_a, before_b, after_a, after_b):
    part = pl.BlockSpec((BLOCK, 512), lambda j: (j, 0))
    full = pl.BlockSpec((BLOCK, WIDTH), lambda j: (j, 0))
    return pl.pallas_call(
        last_sum_kernel,
        grid=(4,),
        in_specs=[full, part, part, part, part],
        out_specs=full,
        out_shape=jax.ShapeDtypeStruct((ROWS, WIDTH), jnp.bfloat16),
        compiler_params=PARAMS,
        cost_estimate=lasting(2),
        name="last_sum",
    )(own, before_a, before_b, after_a, after_b)


def scalar_table(doc_start, balanced_source):
    device = lax.axis_index("cp")
    member = device % GROUP
    group_blocks = GROUP * BLK_DEV
    group_first = device // GROUP * group_blocks
    sources = lax.dynamic_slice_in_dim(balanced_source, group_first, group_blocks) - group_first
    slots = jnp.arange(group_blocks, dtype=jnp.int32)
    slot_of = jnp.sum(
        jnp.where(sources[None, :] == slots[:, None], slots[None, :], 0), axis=1, dtype=jnp.int32
    )
    mine = member * BLK_DEV
    wanted = lax.dynamic_slice_in_dim(sources, mine, BLK_DEV)
    held = lax.dynamic_slice_in_dim(slot_of, mine, BLK_DEV)
    starts = lax.dynamic_slice_in_dim(doc_start, device * BLK_DEV, BLK_DEV)
    starts = starts - (device * BLK_DEV - PRIOR)
    return jnp.concatenate(
        [
            starts,
            (held // BLK_DEV) ^ member,
            held % BLK_DEV,
            (wanted // BLK_DEV) ^ member,
            wanted % BLK_DEV,
            jnp.stack([device % 2, lax.axis_index("tp")]),
        ]
    ).astype(jnp.int32)


def group_exchange(block, earlier):
    across = swap_cp(block, 2)
    return [block, swap_cp(after(block, earlier), 1), across, swap_cp(after(across, earlier), 1)]


def copy_all(*pairs, sems):
    copies = [pltpu.make_async_copy(src, dst, sems.at[at]) for at, (src, dst) in enumerate(pairs)]
    for copy in copies:
        copy.start()
    for copy in copies:
        copy.wait()


def join_kernel(keys, values, kv, last, sems):
    tail = pl.ds(ROWS - FAR_ROWS, FAR_ROWS)
    left, right = pl.ds(0, HD), pl.ds(HD, HD)
    copy_all(
        (keys, kv.at[:, left]),
        (values, kv.at[:, right]),
        (keys.at[tail], last.at[:, left]),
        (values.at[tail], last.at[:, right]),
        sems=sems,
    )


def join(keys, values):
    return pl.pallas_call(
        join_kernel,
        in_specs=[HBM] * 2,
        out_specs=[WHOLE] * 2,
        out_shape=[
            jax.ShapeDtypeStruct((ROWS, 2 * HD), jnp.bfloat16),
            jax.ShapeDtypeStruct((FAR_ROWS, 2 * HD), jnp.bfloat16),
        ],
        scratch_shapes=[pltpu.SemaphoreType.DMA((4,))],
        compiler_params=PARAMS,
        cost_estimate=lasting(2),
        name="join",
    )(keys, values)


def halve_kernel(before, ahead, upper, lower, sems):
    half = ROWS // 2
    copy_all((before.at[pl.ds(0, half)], upper), (ahead.at[pl.ds(half, half)], lower), sems=sems)


def halve(before, ahead):
    return pl.pallas_call(
        halve_kernel,
        in_specs=[ANY] * 2,
        out_specs=[WHOLE] * 2,
        out_shape=[jax.ShapeDtypeStruct((ROWS // 2, WIDTH), jnp.bfloat16)] * 2,
        scratch_shapes=[pltpu.SemaphoreType.DMA((2,))],
        compiler_params=PARAMS,
        cost_estimate=lasting(1),
        name="halve",
    )(before, ahead)


def add_kernel(own, near, far, keys, values):
    total = own[...] + near[...].astype(jnp.float32)
    front = total[: ROWS - FAR_ROWS].astype(jnp.bfloat16)
    rear = (total[ROWS - FAR_ROWS :] + far[...].astype(jnp.float32)).astype(jnp.bfloat16)
    for col, out in ((0, keys), (HD, values)):
        out[: ROWS - FAR_ROWS] = front[:, col : col + HD]
        out[ROWS - FAR_ROWS :] = rear[:, col : col + HD]


def add_terms(own, near, far):
    return pl.pallas_call(
        add_kernel,
        in_specs=[WHOLE] * 3,
        out_specs=[WHOLE] * 2,
        out_shape=[jax.ShapeDtypeStruct((ROWS, HD), jnp.bfloat16)] * 2,
        compiler_params=PARAMS,
        cost_estimate=lasting(1),
        name="add_terms",
    )(own, near, far)


def after(value, earlier):
    return lax.optimization_barrier((value, earlier))[0]


def shards(queries, key_rows, value_rows, out_proj, grad_mixed, doc_start, balanced_source):
    table = scalar_table(doc_start, balanced_source)

    kv, last = join(key_rows, value_rows)
    far = shift_cp(last, 2)
    near = shift_cp(kv, 1)
    pool = (kv, far, near)

    grads_in = after(grad_mixed, kv)
    grads_before = shift_tp(grads_in, 1)
    grads_ahead = shift_tp(grads_in, -1)

    attended, attended_t, totals = [], [], []
    for chunk in range(CHUNKS):
        att, att_t, total, *laid_out = forward(
            after(table, (attended[0], upper, lower))
            if chunk
            else table,
            queries,
            pool,
            chunk,
        )
        if chunk == 0:
            pool = laid_out
            upper, lower = halve(after(grads_before, att), grads_ahead)
        attended.append(att)
        attended_t.append(att_t)
        totals.append(total)

    pieces = (grad_mixed, grads_ahead, shift_tp(upper, 1), shift_tp(lower, -1), grads_before)
    exchanged = [group_exchange(attended[0], attended[1]), None]
    grad_attended = grad_matmul(table, pieces, out_proj)
    exchanged[1] = group_exchange(attended[1], grad_attended[1])
    grad_across = swap_cp(grad_attended[0], 2)

    far_left, far_right, onward_b, back_a, own, rows = products(
        after(table, grad_attended[1]), exchanged, out_proj
    )
    from_before = shift_tp(far_left, 1)
    from_after = shift_tp(far_right, -1)

    grad_sources = [
        [
            grad_attended[0],
            swap_cp(after(grad_attended[0], own), 1),
            grad_across,
            swap_cp(after(grad_across, own), 1),
        ]
    ]
    swapped = swap_cp(grad_attended[1], 1)
    carried = backward(
        after(table, (own, swapped)),
        queries, attended_t[0], totals[0], pool, grad_sources[0], None, 0, False,
    )
    query_a = carried[1]
    across = swap_cp(after(grad_attended[1], grad_across), 2)
    grad_sources.append(
        [
            grad_attended[1],
            swapped,
            across,
            swap_cp(after(across, query_a), 1),
        ]
    )
    before_b = shift_tp(onward_b, 1)
    after_a = shift_tp(back_a, -1)
    onward_a, back_b = sum_products(
        after(table, query_a), rows, out_proj, from_before, from_after)
    before_a = shift_tp(onward_a, 1)
    after_b = shift_tp(back_b, -1)
    query_grad, own_grads, near_grads, far_grads = backward(
        after(table, onward_a),
        queries, attended_t[1], totals[1], pool, grad_sources[1], carried, 1, True,
    )
    far_back = shift_cp(after(far_grads, (before_b, after_a)), -2)
    near_back = shift_cp(after(near_grads, (before_b, after_a)), -1)
    mixed = last_sum(own, before_a, before_b, after_a, after_b)
    key_grad, value_grad = add_terms(after(own_grads, mixed), near_back, far_back)
    return (mixed, query_grad, key_grad, value_grad)


def solution(mesh):
    placed = (P("cp", "tp"), P("cp", "tp"), P("cp", "tp"), P("tp", None), P("cp", "tp"), P(), P())
    return jax.shard_map(
        shards,
        mesh=mesh,
        in_specs=placed,
        out_specs=(P("cp", "tp"),) * 4,
        check_vma=False,
    )
```

```python
import math

import jax
import jax.numpy as jnp
from jax import lax
from jax.experimental import pallas as pl
from jax.experimental.pallas import tpu as pltpu
from jax.sharding import PartitionSpec as P

HD = 128
BLOCK = 128
BLK_DEV = 4
MAXB = 8
GROUP = 4
PRIOR = MAXB - 1
POOL = PRIOR + BLK_DEV
ROWS = BLOCK * BLK_DEV
WIDTH = 1024
FAR_ROWS = (PRIOR - BLK_DEV) * BLOCK
CHUNKS = 2
CW = WIDTH // CHUNKS
FW = 512
BW = 512

SCALE = 1.0 / math.sqrt(HD)
SCALE_LOG2 = SCALE * math.log2(math.e)
MASKED = -1e30

START, GRAD_REL, GRAD_IDX, ATT_REL, ATT_IDX, CORE, TP = 0, 4, 8, 12, 16, 20, 21

ANY = pl.BlockSpec(memory_space=pl.ANY)
WHOLE = pl.BlockSpec(memory_space=pltpu.VMEM)
HBM = pl.BlockSpec(memory_space=pltpu.HBM)
SMEM = pl.BlockSpec(memory_space=pltpu.SMEM)
VMEM_LIMIT = 48 * 1024 * 1024


PARAMS = pltpu.CompilerParams(vmem_limit_bytes=VMEM_LIMIT)


def lasting(us):
    return pl.CostEstimate(
        flops=int(us * 1.15e9), bytes_accessed=int(us * 3.6e6), transcendentals=0
    )


def dot(a, b):
    return jnp.dot(a, b, preferred_element_type=jnp.float32)


def dot_nt(a, b):
    return lax.dot_general(a, b, (((1,), (1,)), ((), ())), preferred_element_type=jnp.float32)


def swap_cp(block, mask):
    count = lax.axis_size("cp")
    return lax.ppermute(block, "cp", [(i, i ^ mask) for i in range(count)])


def shift_cp(block, distance):
    count = lax.axis_size("cp")
    route = [(i, i + distance) for i in range(count) if 0 <= i + distance < count]
    return lax.ppermute(block, "cp", route)


def shift_tp(block, distance):
    count = lax.axis_size("tp")
    return lax.ppermute(block, "tp", [(i, (i + distance) % count) for i in range(count)])


def pool_copies(kv, far, near, keys, values, sems):
    copies = []
    for src, row, rows, place in (
        (kv, 0, ROWS, PRIOR * BLOCK),
        (far, 0, FAR_ROWS, 0),
        (near, 0, ROWS, ROWS - BLOCK),
    ):
        for col, pool in ((0, keys), (HD, values)):
            copies.append(
                pltpu.make_async_copy(
                    src.at[pl.ds(row, rows), pl.ds(col, HD)],
                    pool.at[pl.ds(place, rows)],
                    sems.at[len(copies)],
                )
            )
    return copies


def block_rows(b):
    return pl.ds(pl.multiple_of(b * BLOCK, BLOCK), BLOCK)


def first_mask(odd, width):
    key_pos = lax.broadcasted_iota(jnp.int32, (256, width), 0)
    row_pos = lax.broadcasted_iota(jnp.int32, (256, width), 1) % BLOCK + BLOCK
    return (key_pos <= row_pos) & (key_pos >= odd * BLOCK)


def flipped_heads(block):
    heads = block.shape[1] // HD
    return jnp.concatenate([block[:, h * HD : (h + 1) * HD].T for h in range(heads)], axis=1)


def stacked_heads(block):
    heads = block.shape[1] // HD
    return jnp.concatenate([block[:, h * HD : (h + 1) * HD] for h in range(heads)], axis=0)


def tiles_of(table, b):
    diag = PRIOR + b
    count = diag - jnp.maximum(table[START + b], 0) + 1
    return (count + 1) // 2, count % 2, diag


def low_of(step, odd, diag):
    block = diag - 1 - 2 * step + jnp.where(step > 0, odd, 0)
    return pl.multiple_of(block * BLOCK, BLOCK)


def forward_kernel(
    chunk, table, q_ref, *refs
):
    if chunk == 0:
        kv, far, near, att, att_t, total_ref, keys, values, sems = refs
        copies = pool_copies(kv, far, near, keys, values, sems)
        for copy in copies:
            copy.start()
        for copy in copies:
            copy.wait()
    else:
        keys, values, att, att_t, total_ref = refs

    groups = [slice(at, at + FW) for at in range(0, CW, FW)]

    def block(b, _):
        steps, odd, diag = tiles_of(table, b)
        q_t = [
            flipped_heads(q_ref[block_rows(b), chunk * CW + cols.start : chunk * CW + cols.stop])
            for cols in groups
        ]

        def tile(step, mask, carry):
            low = low_of(step, odd, diag)
            k = keys[pl.ds(low, 256), :]
            v_t = values[pl.ds(low, 256), :].T
            result = []
            for at in range(len(groups)):
                s = dot(k, q_t[at]) * SCALE_LOG2
                if carry is None:
                    s = jnp.where(mask, s, MASKED)
                    top = jnp.max(s, axis=0, keepdims=True)
                    p = jnp.exp2(s - top)
                    total = jnp.sum(p, axis=0, keepdims=True)
                    acc = dot(v_t, p.astype(jnp.bfloat16))
                else:
                    top_old, total, acc = carry[at]
                    top = jnp.maximum(top_old, jnp.max(s, axis=0, keepdims=True))
                    fade = jnp.exp2(top_old - top)
                    p = jnp.exp2(s - top)
                    total = total * fade + jnp.sum(p, axis=0, keepdims=True)
                    acc = acc * fade + dot(v_t, p.astype(jnp.bfloat16))
                result.append((top, total, acc))
            return result

        carry = tile(0, first_mask(odd, FW), None)
        carry = lax.fori_loop(1, steps, lambda step, carry: tile(step, None, carry), carry)
        for cols, (top, total, acc) in zip(groups, carry):
            out = (acc * (1.0 / total)).astype(jnp.bfloat16)
            att_t[b, :, cols] = out
            for head in range(FW // HD):
                at = cols.start + head * HD
                att[block_rows(b), at : at + HD] = out[:, head * HD : (head + 1) * HD].T
            total_ref[b, :, cols] = top + jnp.log2(total)
        return _

    lax.fori_loop(0, BLK_DEV, block, 0)


def forward(table, queries, pool, chunk):
    first = chunk == 0
    pool_shape = jax.ShapeDtypeStruct((POOL * BLOCK, HD), jnp.bfloat16)

    def kernel(*refs):
        forward_kernel(chunk, *refs)

    return pl.pallas_call(
        kernel,
        in_specs=[SMEM, WHOLE] + ([ANY] * 3 if first else [WHOLE] * 2),
        out_specs=[WHOLE] * (5 if first else 3),
        out_shape=[
            jax.ShapeDtypeStruct((ROWS, CW), jnp.bfloat16),
            jax.ShapeDtypeStruct((BLK_DEV, HD, CW), jnp.bfloat16),
            jax.ShapeDtypeStruct((BLK_DEV, 1, CW), jnp.float32),
        ]
        + ([pool_shape] * 2 if first else []),
        scratch_shapes=[pltpu.SemaphoreType.DMA((6,))] if first else [],
        compiler_params=PARAMS,
        cost_estimate=lasting(8),
        name="attention_forward",
    )(table, queries, *pool)


def start_chosen(rel, index, sources, place, sem, col=0):
    for at, source in enumerate(sources):
        @pl.when(rel == at)
        def _():
            pltpu.make_async_copy(
                source.at[pl.ds(pl.multiple_of(index * BLOCK, BLOCK), BLOCK)], place, sem
            ).start()


def backward_kernel(chunk, last, first, *refs):
    refs = list(refs)
    table, q_ref, att_t, total_ref, keys, values = refs[:6]
    sources = refs[6:10]
    refs = refs[10:]
    if not first:
        key_in, value_in = refs[1:3]
        refs = refs[3:]
    dq_hbm = refs[0]
    if last:
        own_ref, near_ref, far_ref = refs[1:4]
        refs = refs[4:]
        key_acc, value_acc = refs[:2]
    else:
        key_acc, value_acc = refs[1:3]
        refs = refs[3:]
    grads, dq, grad_sems, out_sems = refs[-4:]

    for at in range(BLK_DEV):
        start_chosen(
            table[GRAD_REL + at], table[GRAD_IDX + at], sources, grads.at[block_rows(at)], grad_sems.at[at]
        )
    key_acc[...] = jnp.zeros_like(key_acc)
    value_acc[...] = jnp.zeros_like(value_acc)
    for at in range(BLK_DEV):
        pltpu.make_async_copy(
            sources[0].at[pl.ds(0, BLOCK)], grads.at[block_rows(at)], grad_sems.at[at]
        ).wait()

    def outward(b):
        return pltpu.make_async_copy(
            dq.at[block_rows(b)], dq_hbm.at[block_rows(b), pl.ds(chunk * CW, CW)], out_sems.at[b]
        )

    groups = [slice(at, at + BW) for at in range(0, CW, BW)]

    def block(b, _):
        steps, odd, diag = tiles_of(table, b)
        held = []
        for cols in groups:
            q = q_ref[block_rows(b), chunk * CW + cols.start : chunk * CW + cols.stop]
            g = grads[block_rows(b), cols]
            g_t = flipped_heads(g)
            delta = jnp.sum(
                g_t.astype(jnp.float32) * att_t[b, :, cols].astype(jnp.float32),
                axis=0,
                keepdims=True,
            )
            held.append(
                (flipped_heads(q), stacked_heads(q), g_t, stacked_heads(g), delta, total_ref[b, :, cols])
            )

        def tile(step, mask, carry):
            low = low_of(step, odd, diag)
            k = keys[pl.ds(low, 256), :]
            k_t = k.T
            v = values[pl.ds(low, 256), :]
            result = []
            key_part = value_part = None
            for at, (q_t, q_s, g_t, g_s, delta, log_total) in enumerate(held):
                s = dot(k, q_t) * SCALE_LOG2
                if mask is not None:
                    s = jnp.where(mask, s, MASKED)
                p = jnp.exp2(s - log_total).astype(jnp.bfloat16)
                dp = dot(v, g_t)
                ds = (p.astype(jnp.float32) * (dp - delta)).astype(jnp.bfloat16)
                value_term, key_term, query_term = dot(p, g_s), dot(ds, q_s), dot(k_t, ds)
                value_part = value_term if value_part is None else value_part + value_term
                key_part = key_term if key_part is None else key_part + key_term
                result.append(query_term if carry is None else carry[at] + query_term)
            value_acc[pl.ds(low, 256), :] += value_part
            key_acc[pl.ds(low, 256), :] += key_part
            return result

        carry = tile(0, first_mask(odd, BW), None)
        carry = lax.fori_loop(1, steps, lambda step, carry: tile(step, None, carry), carry)
        for cols, dq_t in zip(groups, carry):
            dq_t = (dq_t * SCALE).astype(jnp.bfloat16)
            for head in range(BW // HD):
                at = cols.start + head * HD
                dq[block_rows(b), at : at + HD] = dq_t[:, head * HD : (head + 1) * HD].T
        outward(b).start()
        return _

    lax.fori_loop(0, BLK_DEV, block, 0)

    if last:
        near_at = ROWS - BLOCK
        own_at = PRIOR * BLOCK
        for acc, earlier, cols, factor in (
            (key_acc, key_in, slice(0, HD), SCALE),
            (value_acc, value_in, slice(HD, 2 * HD), 1.0),
        ):
            def total(rows):
                return (acc[rows] + earlier[rows]) * factor

            far_ref[:, cols] = total(slice(0, near_at)).astype(jnp.bfloat16)
            near_ref[:, cols] = total(slice(near_at, own_at)).astype(jnp.bfloat16)
            own_ref[:, cols] = total(slice(own_at, None))
    for b in range(BLK_DEV):
        outward(b).wait()


def backward(table, queries, att_t, totals, pool, sources, carried, chunk, last):
    first = carried is None
    pool_shape = (POOL * BLOCK, HD)
    sums = [jax.ShapeDtypeStruct(pool_shape, jnp.float32)] * 2
    if last:
        out_shape = [
            jax.ShapeDtypeStruct((ROWS, 2 * HD), jnp.float32),
            jax.ShapeDtypeStruct((ROWS, 2 * HD), jnp.bfloat16),
            jax.ShapeDtypeStruct((FAR_ROWS, 2 * HD), jnp.bfloat16),
        ]
        scratch = [pltpu.VMEM(pool_shape, jnp.float32)] * 2
    else:
        out_shape, scratch = sums, []

    def kernel(*refs):
        backward_kernel(chunk, last, first, *refs)

    return pl.pallas_call(
        kernel,
        in_specs=[SMEM] + [WHOLE] * 5 + [ANY] * 4 + ([] if first else [ANY, WHOLE, WHOLE]),
        out_specs=[ANY] + [WHOLE] * len(out_shape),
        out_shape=[jax.ShapeDtypeStruct((ROWS, WIDTH), jnp.bfloat16)] + out_shape,
        input_output_aliases={} if first else {10: 0},
        scratch_shapes=scratch
        + [
            pltpu.VMEM((ROWS, CW), jnp.bfloat16),
            pltpu.VMEM((ROWS, CW), jnp.bfloat16),
            pltpu.SemaphoreType.DMA((BLK_DEV,)),
            pltpu.SemaphoreType.DMA((BLK_DEV,)),
        ],
        compiler_params=PARAMS,
        cost_estimate=lasting(9),
        name="attention_backward",
    )(table, queries, att_t, totals, *pool, *sources, *([] if first else carried))


def grad_matmul_kernel(table, *refs):
    pieces, weight_hbm, outs = refs[:8], refs[8], refs[9 : 9 + CHUNKS]
    weight, sems = refs[9 + CHUNKS :]
    half = ROWS // 2
    copies = []
    for chunk in range(CHUNKS):
        for ahead in range(4):
            at = pl.multiple_of(((table[TP] + ahead) % 4) * WIDTH, WIDTH)
            copies.append(
                pltpu.make_async_copy(
                    weight_hbm.at[pl.ds(chunk * CW, CW), pl.ds(at, WIDTH)],
                    weight.at[4 * chunk + ahead],
                    sems.at[4 * chunk + ahead],
                )
            )
            copies[-1].start()
    for chunk in range(CHUNKS):
        totals = [None, None]
        for ahead in range(4):
            slot = 4 * chunk + ahead
            copies[slot].wait()
            for part in range(2):
                term = dot_nt(pieces[2 * ahead + part][...], weight[slot])
                totals[part] = term if totals[part] is None else totals[part] + term
        for part in range(2):
            outs[chunk][part * half : (part + 1) * half] = totals[part].astype(jnp.bfloat16)


def grad_matmul(table, pieces, weight):
    return pl.pallas_call(
        grad_matmul_kernel,
        in_specs=[SMEM] + [WHOLE] * 8 + [ANY],
        out_specs=[WHOLE] * CHUNKS,
        out_shape=[jax.ShapeDtypeStruct((ROWS, CW), jnp.bfloat16)] * CHUNKS,
        scratch_shapes=[
            pltpu.VMEM((4 * CHUNKS, CW, WIDTH), jnp.bfloat16),
            pltpu.SemaphoreType.DMA((4 * CHUNKS,)),
        ],
        compiler_params=PARAMS,
        cost_estimate=lasting(7),
        name="grad_projection",
    )(table, *pieces, weight)


HALF = WIDTH // 2


def weight_copy(table, weight_hbm, weight, slot, ahead, half, sem):
    at = pl.multiple_of(((table[TP] + ahead) % 4) * WIDTH + half * HALF, HALF)
    return pltpu.make_async_copy(weight_hbm.at[:, pl.ds(at, HALF)], weight.at[slot], sem)


def product_kernel(table, *refs):
    sources = [refs[4 * c : 4 * c + 4] for c in range(CHUNKS)]
    weight_hbm, left, right, onward, back, own, rows, weight, sems, weight_sems = refs[4 * CHUNKS :]

    def place(c, at):
        return rows.at[block_rows(at), pl.ds(c * CW, CW)]

    places = [(c, at, c * BLK_DEV + at) for c in range(CHUNKS) for at in range(BLK_DEV)]
    for c, at, sem in places:
        start_chosen(
            table[ATT_REL + at], table[ATT_IDX + at], sources[c], place(c, at), sems.at[sem]
        )
    parts = ((2, 0), (2, 1), (1, 1), (3, 0), (0, 0), (0, 1))
    weights = [
        weight_copy(table, weight_hbm, weight, slot, ahead, half, weight_sems.at[slot])
        for slot, (ahead, half) in enumerate(parts)
    ]
    for copy in weights:
        copy.start()
    for c, at, sem in places:
        pltpu.make_async_copy(sources[c][0].at[pl.ds(0, BLOCK)], place(c, at), sems.at[sem]).wait()
    for slot, out in enumerate((left, right, onward, back)):
        weights[slot].wait()
        out[...] = dot(rows[...], weight[slot]).astype(jnp.bfloat16)
    for slot in (4, 5):
        weights[slot].wait()
        own[:, (slot - 4) * HALF : (slot - 3) * HALF] = dot(rows[...], weight[slot]).astype(
            jnp.bfloat16
        )


def products(table, sources, weight):
    flat = [source for group in sources for source in group]
    return pl.pallas_call(
        product_kernel,
        in_specs=[SMEM] + [ANY] * (4 * CHUNKS + 1),
        out_specs=[WHOLE] * 6,
        out_shape=[jax.ShapeDtypeStruct((ROWS, HALF), jnp.bfloat16)] * 4
        + [jax.ShapeDtypeStruct((ROWS, WIDTH), jnp.bfloat16)] * 2,
        scratch_shapes=[
            pltpu.VMEM((6, WIDTH, HALF), jnp.bfloat16),
            pltpu.SemaphoreType.DMA((4 * CHUNKS,)),
            pltpu.SemaphoreType.DMA((6,)),
        ],
        compiler_params=PARAMS,
        cost_estimate=lasting(7),
        name="products",
    )(table, *flat, weight)


def sum_product_kernel(table, rows, weight_hbm, before, after_, onward, back, weight, sems):
    weights = [
        weight_copy(table, weight_hbm, weight, 0, 1, 0, sems.at[0]),
        weight_copy(table, weight_hbm, weight, 1, 3, 1, sems.at[1]),
    ]
    for copy in weights:
        copy.start()
    for slot, (extra, out) in enumerate(((before, onward), (after_, back))):
        weights[slot].wait()
        value = dot(rows[...], weight[slot])
        out[...] = (value + extra[...].astype(jnp.float32)).astype(jnp.bfloat16)


def sum_products(table, rows, weight, before, after):
    half = jax.ShapeDtypeStruct((ROWS, HALF), jnp.bfloat16)
    return pl.pallas_call(
        sum_product_kernel,
        in_specs=[SMEM, WHOLE, ANY, WHOLE, WHOLE],
        out_specs=[WHOLE] * 2,
        out_shape=[half] * 2,
        scratch_shapes=[
            pltpu.VMEM((2, WIDTH, HALF), jnp.bfloat16),
            pltpu.SemaphoreType.DMA((2,)),
        ],
        compiler_params=PARAMS,
        cost_estimate=lasting(4),
        name="sum_products",
    )(table, rows, weight, before, after)


def last_sum_kernel(own, before_a, before_b, after_a, after_b, out):
    for half, before, after in ((0, before_a, after_a), (1, before_b, after_b)):
        cols = slice(half * 512, (half + 1) * 512)
        out[:, cols] = (
            own[:, cols].astype(jnp.float32) + before[...].astype(jnp.float32) + after[...].astype(jnp.float32)
        ).astype(jnp.bfloat16)


def last_sum(own, before_a, before_b, after_a, after_b):
    part = pl.BlockSpec((BLOCK, 512), lambda j: (j, 0))
    full = pl.BlockSpec((BLOCK, WIDTH), lambda j: (j, 0))
    return pl.pallas_call(
        last_sum_kernel,
        grid=(4,),
        in_specs=[full, part, part, part, part],
        out_specs=full,
        out_shape=jax.ShapeDtypeStruct((ROWS, WIDTH), jnp.bfloat16),
        compiler_params=PARAMS,
        cost_estimate=lasting(2),
        name="last_sum",
    )(own, before_a, before_b, after_a, after_b)


def scalar_table(doc_start, balanced_source):
    device = lax.axis_index("cp")
    member = device % GROUP
    group_blocks = GROUP * BLK_DEV
    group_first = device // GROUP * group_blocks
    sources = lax.dynamic_slice_in_dim(balanced_source, group_first, group_blocks) - group_first
    slots = jnp.arange(group_blocks, dtype=jnp.int32)
    slot_of = jnp.sum(
        jnp.where(sources[None, :] == slots[:, None], slots[None, :], 0), axis=1, dtype=jnp.int32
    )
    mine = member * BLK_DEV
    wanted = lax.dynamic_slice_in_dim(sources, mine, BLK_DEV)
    held = lax.dynamic_slice_in_dim(slot_of, mine, BLK_DEV)
    starts = lax.dynamic_slice_in_dim(doc_start, device * BLK_DEV, BLK_DEV)
    starts = starts - (device * BLK_DEV - PRIOR)
    return jnp.concatenate(
        [
            starts,
            (held // BLK_DEV) ^ member,
            held % BLK_DEV,
            (wanted // BLK_DEV) ^ member,
            wanted % BLK_DEV,
            jnp.stack([device % 2, lax.axis_index("tp")]),
        ]
    ).astype(jnp.int32)


def group_exchange(block, earlier):
    across = swap_cp(block, 2)
    return [block, swap_cp(after(block, earlier), 1), across, swap_cp(after(across, earlier), 1)]


def copy_all(*pairs, sems):
    copies = [pltpu.make_async_copy(src, dst, sems.at[at]) for at, (src, dst) in enumerate(pairs)]
    for copy in copies:
        copy.start()
    for copy in copies:
        copy.wait()


def join_kernel(keys, values, grads, kv, last, upper, lower, sems):
    half = ROWS // 2
    tail = pl.ds(ROWS - FAR_ROWS, FAR_ROWS)
    left, right = pl.ds(0, HD), pl.ds(HD, HD)
    copy_all(
        (keys, kv.at[:, left]),
        (values, kv.at[:, right]),
        (keys.at[tail], last.at[:, left]),
        (values.at[tail], last.at[:, right]),
        (grads.at[pl.ds(0, half)], upper),
        (grads.at[pl.ds(half, half)], lower),
        sems=sems,
    )


def join(keys, values, grads):
    return pl.pallas_call(
        join_kernel,
        in_specs=[HBM] * 3,
        out_specs=[WHOLE] * 4,
        out_shape=[
            jax.ShapeDtypeStruct((ROWS, 2 * HD), jnp.bfloat16),
            jax.ShapeDtypeStruct((FAR_ROWS, 2 * HD), jnp.bfloat16),
        ]
        + [jax.ShapeDtypeStruct((ROWS // 2, WIDTH), jnp.bfloat16)] * 2,
        scratch_shapes=[pltpu.SemaphoreType.DMA((6,))],
        compiler_params=PARAMS,
        cost_estimate=lasting(2),
        name="join",
    )(keys, values, grads)


def add_kernel(own, near, far, keys, values):
    total = own[...] + near[...].astype(jnp.float32)
    front = total[: ROWS - FAR_ROWS].astype(jnp.bfloat16)
    rear = (total[ROWS - FAR_ROWS :] + far[...].astype(jnp.float32)).astype(jnp.bfloat16)
    for col, out in ((0, keys), (HD, values)):
        out[: ROWS - FAR_ROWS] = front[:, col : col + HD]
        out[ROWS - FAR_ROWS :] = rear[:, col : col + HD]


def add_terms(own, near, far):
    return pl.pallas_call(
        add_kernel,
        in_specs=[WHOLE] * 3,
        out_specs=[WHOLE] * 2,
        out_shape=[jax.ShapeDtypeStruct((ROWS, HD), jnp.bfloat16)] * 2,
        compiler_params=PARAMS,
        cost_estimate=lasting(1),
        name="add_terms",
    )(own, near, far)


def after(value, earlier):
    return lax.optimization_barrier((value, earlier))[0]


def shards(queries, key_rows, value_rows, out_proj, grad_mixed, doc_start, balanced_source):
    table = scalar_table(doc_start, balanced_source)

    kv, last, upper, lower = join(key_rows, value_rows, grad_mixed)
    far = shift_cp(last, 2)
    near = shift_cp(kv, 1)
    pool = (kv, far, near)

    before_upper = shift_tp(upper, 1)
    ahead_lower = shift_tp(lower, -1)
    before_lower = shift_tp(after(lower, far), 1)
    ahead_upper = shift_tp(after(upper, far), -1)

    attended, attended_t, totals = [], [], []
    for chunk in range(CHUNKS):
        att, att_t, total, *laid_out = forward(
            after(table, (attended[0], before_upper, ahead_lower))
            if chunk
            else table,
            queries,
            pool,
            chunk,
        )
        if chunk == 0:
            pool = laid_out
            opposite = [
                shift_tp(after(before_upper, att), 1),
                shift_tp(after(ahead_lower, att), -1),
            ]
        attended.append(att)
        attended_t.append(att_t)
        totals.append(total)

    pieces = (upper, lower, ahead_upper, ahead_lower, *opposite, before_upper, before_lower)
    exchanged = [group_exchange(attended[0], attended[1]), None]
    grad_attended = grad_matmul(table, pieces, out_proj)
    across = swap_cp(after(attended[1], (before_lower, ahead_upper)), 2)
    exchanged[1] = [
        attended[1],
        swap_cp(after(attended[1], grad_attended[1]), 1),
        across,
        swap_cp(after(across, grad_attended[1]), 1),
    ]
    grad_across = swap_cp(grad_attended[0], 2)

    far_left, far_right, onward_b, back_a, own, rows = products(
        after(table, grad_attended[1]), exchanged, out_proj
    )
    from_before = shift_tp(far_left, 1)
    from_after = shift_tp(far_right, -1)

    grad_sources = [
        [
            grad_attended[0],
            swap_cp(after(grad_attended[0], own), 1),
            grad_across,
            swap_cp(after(grad_across, own), 1),
        ]
    ]
    swapped = swap_cp(grad_attended[1], 1)
    carried = backward(
        after(table, (own, swapped)),
        queries, attended_t[0], totals[0], pool, grad_sources[0], None, 0, False,
    )
    query_a = carried[1]
    across = swap_cp(after(grad_attended[1], grad_across), 2)
    grad_sources.append(
        [
            grad_attended[1],
            swapped,
            across,
            swap_cp(after(across, query_a), 1),
        ]
    )
    before_b = shift_tp(onward_b, 1)
    after_a = shift_tp(back_a, -1)
    onward_a, back_b = sum_products(
        after(table, query_a), rows, out_proj, from_before, from_after)
    before_a = shift_tp(onward_a, 1)
    after_b = shift_tp(back_b, -1)
    query_grad, own_grads, near_grads, far_grads = backward(
        after(table, onward_a),
        queries, attended_t[1], totals[1], pool, grad_sources[1], carried, 1, True,
    )
    far_back = shift_cp(after(far_grads, (before_b, after_a)), -2)
    near_back = shift_cp(after(near_grads, (before_b, after_a)), -1)
    mixed = last_sum(own, before_a, before_b, after_a, after_b)
    key_grad, value_grad = add_terms(after(own_grads, mixed), near_back, far_back)
    return (mixed, query_grad, key_grad, value_grad)


def solution(mesh):
    placed = (P("cp", "tp"), P("cp", "tp"), P("cp", "tp"), P("tp", None), P("cp", "tp"), P(), P())
    return jax.shard_map(
        shards,
        mesh=mesh,
        in_specs=placed,
        out_specs=(P("cp", "tp"),) * 4,
        check_vma=False,
    )
```

```python
import math

import jax
import jax.numpy as jnp
from jax import lax
from jax.experimental import pallas as pl
from jax.experimental.pallas import tpu as pltpu
from jax.sharding import PartitionSpec as P

HD = 128
BLOCK = 128
BLK_DEV = 4
MAXB = 8
GROUP = 4
PRIOR = MAXB - 1
POOL = PRIOR + BLK_DEV
ROWS = BLOCK * BLK_DEV
WIDTH = 1024
FAR_ROWS = (PRIOR - BLK_DEV) * BLOCK
CHUNKS = 2
CW = WIDTH // CHUNKS
FW = 512
BW = 512

SCALE = 1.0 / math.sqrt(HD)
SCALE_LOG2 = SCALE * math.log2(math.e)
MASKED = -1e30

START, GRAD_REL, GRAD_IDX, ATT_REL, ATT_IDX, CORE, TP = 0, 4, 8, 12, 16, 20, 21

ANY = pl.BlockSpec(memory_space=pl.ANY)
WHOLE = pl.BlockSpec(memory_space=pltpu.VMEM)
HBM = pl.BlockSpec(memory_space=pltpu.HBM)
SMEM = pl.BlockSpec(memory_space=pltpu.SMEM)
VMEM_LIMIT = 48 * 1024 * 1024


PARAMS = pltpu.CompilerParams(vmem_limit_bytes=VMEM_LIMIT)


def lasting(us):
    return pl.CostEstimate(
        flops=int(us * 1.15e9), bytes_accessed=int(us * 3.6e6), transcendentals=0
    )


def dot(a, b):
    return jnp.dot(a, b, preferred_element_type=jnp.float32)


def dot_nt(a, b):
    return lax.dot_general(a, b, (((1,), (1,)), ((), ())), preferred_element_type=jnp.float32)


def swap_cp(block, mask):
    count = lax.axis_size("cp")
    return lax.ppermute(block, "cp", [(i, i ^ mask) for i in range(count)])


def shift_cp(block, distance):
    count = lax.axis_size("cp")
    route = [(i, i + distance) for i in range(count) if 0 <= i + distance < count]
    return lax.ppermute(block, "cp", route)


def shift_tp(block, distance):
    count = lax.axis_size("tp")
    return lax.ppermute(block, "tp", [(i, (i + distance) % count) for i in range(count)])


def pool_copies(kv, far, near, keys, values, sems):
    copies = []
    for src, row, rows, place in (
        (kv, 0, ROWS, PRIOR * BLOCK),
        (far, 0, FAR_ROWS, 0),
        (near, 0, ROWS, ROWS - BLOCK),
    ):
        for col, pool in ((0, keys), (HD, values)):
            copies.append(
                pltpu.make_async_copy(
                    src.at[pl.ds(row, rows), pl.ds(col, HD)],
                    pool.at[pl.ds(place, rows)],
                    sems.at[len(copies)],
                )
            )
    return copies


def block_rows(b):
    return pl.ds(pl.multiple_of(b * BLOCK, BLOCK), BLOCK)


def first_mask(odd, width):
    key_pos = lax.broadcasted_iota(jnp.int32, (256, width), 0)
    row_pos = lax.broadcasted_iota(jnp.int32, (256, width), 1) % BLOCK + BLOCK
    return (key_pos <= row_pos) & (key_pos >= odd * BLOCK)


def flipped_heads(block):
    heads = block.shape[1] // HD
    return jnp.concatenate([block[:, h * HD : (h + 1) * HD].T for h in range(heads)], axis=1)


def stacked_heads(block):
    heads = block.shape[1] // HD
    return jnp.concatenate([block[:, h * HD : (h + 1) * HD] for h in range(heads)], axis=0)


def tiles_of(table, b):
    diag = PRIOR + b
    count = diag - jnp.maximum(table[START + b], 0) + 1
    return (count + 1) // 2, count % 2, diag


def low_of(step, odd, diag):
    block = diag - 1 - 2 * step + jnp.where(step > 0, odd, 0)
    return pl.multiple_of(block * BLOCK, BLOCK)


def forward_kernel(
    chunk, table, q_ref, *refs
):
    if chunk == 0:
        kv, far, near, att, att_t, total_ref, keys, values, sems = refs
        copies = pool_copies(kv, far, near, keys, values, sems)
        for copy in copies:
            copy.start()
        for copy in copies:
            copy.wait()
    else:
        keys, values, att, att_t, total_ref = refs

    groups = [slice(at, at + FW) for at in range(0, CW, FW)]

    def block(b, _):
        steps, odd, diag = tiles_of(table, b)
        q_t = [
            flipped_heads(q_ref[block_rows(b), chunk * CW + cols.start : chunk * CW + cols.stop])
            for cols in groups
        ]

        def tile(step, mask, carry):
            low = low_of(step, odd, diag)
            k = keys[pl.ds(low, 256), :]
            v_t = values[pl.ds(low, 256), :].T
            result = []
            for at in range(len(groups)):
                s = dot(k, q_t[at]) * SCALE_LOG2
                if carry is None:
                    s = jnp.where(mask, s, MASKED)
                    top = jnp.max(s, axis=0, keepdims=True)
                    p = jnp.exp2(s - top)
                    total = jnp.sum(p, axis=0, keepdims=True)
                    acc = dot(v_t, p.astype(jnp.bfloat16))
                else:
                    top_old, total, acc = carry[at]
                    top = jnp.maximum(top_old, jnp.max(s, axis=0, keepdims=True))
                    fade = jnp.exp2(top_old - top)
                    p = jnp.exp2(s - top)
                    total = total * fade + jnp.sum(p, axis=0, keepdims=True)
                    acc = acc * fade + dot(v_t, p.astype(jnp.bfloat16))
                result.append((top, total, acc))
            return result

        carry = tile(0, first_mask(odd, FW), None)
        carry = lax.fori_loop(1, steps, lambda step, carry: tile(step, None, carry), carry)
        for cols, (top, total, acc) in zip(groups, carry):
            out = (acc * (1.0 / total)).astype(jnp.bfloat16)
            att_t[b, :, cols] = out
            for head in range(FW // HD):
                at = cols.start + head * HD
                att[block_rows(b), at : at + HD] = out[:, head * HD : (head + 1) * HD].T
            total_ref[b, :, cols] = top + jnp.log2(total)
        return _

    lax.fori_loop(0, BLK_DEV, block, 0)


def forward(table, queries, pool, chunk):
    first = chunk == 0
    pool_shape = jax.ShapeDtypeStruct((POOL * BLOCK, HD), jnp.bfloat16)

    def kernel(*refs):
        forward_kernel(chunk, *refs)

    return pl.pallas_call(
        kernel,
        in_specs=[SMEM, WHOLE] + ([ANY] * 3 if first else [WHOLE] * 2),
        out_specs=[WHOLE] * (5 if first else 3),
        out_shape=[
            jax.ShapeDtypeStruct((ROWS, CW), jnp.bfloat16),
            jax.ShapeDtypeStruct((BLK_DEV, HD, CW), jnp.bfloat16),
            jax.ShapeDtypeStruct((BLK_DEV, 1, CW), jnp.float32),
        ]
        + ([pool_shape] * 2 if first else []),
        scratch_shapes=[pltpu.SemaphoreType.DMA((6,))] if first else [],
        compiler_params=PARAMS,
        cost_estimate=lasting(8),
        name="attention_forward",
    )(table, queries, *pool)


def start_chosen(rel, index, sources, place, sem, col=0):
    for at, source in enumerate(sources):
        @pl.when(rel == at)
        def _():
            pltpu.make_async_copy(
                source.at[pl.ds(pl.multiple_of(index * BLOCK, BLOCK), BLOCK)], place, sem
            ).start()


def backward_kernel(chunk, last, first, *refs):
    refs = list(refs)
    table, q_ref, att_t, total_ref, keys, values = refs[:6]
    sources = refs[6:10]
    refs = refs[10:]
    if not first:
        key_in, value_in = refs[1:3]
        refs = refs[3:]
    dq_hbm = refs[0]
    if last:
        own_ref, near_ref, far_ref = refs[1:4]
        refs = refs[4:]
        key_acc, value_acc = refs[:2]
    else:
        key_acc, value_acc = refs[1:3]
        refs = refs[3:]
    grads, dq, grad_sems, out_sems = refs[-4:]

    for at in range(BLK_DEV):
        start_chosen(
            table[GRAD_REL + at], table[GRAD_IDX + at], sources, grads.at[block_rows(at)], grad_sems.at[at]
        )
    key_acc[...] = jnp.zeros_like(key_acc)
    value_acc[...] = jnp.zeros_like(value_acc)
    for at in range(BLK_DEV):
        pltpu.make_async_copy(
            sources[0].at[pl.ds(0, BLOCK)], grads.at[block_rows(at)], grad_sems.at[at]
        ).wait()

    def outward(b):
        return pltpu.make_async_copy(
            dq.at[block_rows(b)], dq_hbm.at[block_rows(b), pl.ds(chunk * CW, CW)], out_sems.at[b]
        )

    groups = [slice(at, at + BW) for at in range(0, CW, BW)]

    def block(b, _):
        steps, odd, diag = tiles_of(table, b)
        held = []
        for cols in groups:
            q = q_ref[block_rows(b), chunk * CW + cols.start : chunk * CW + cols.stop]
            g = grads[block_rows(b), cols]
            g_t = flipped_heads(g)
            delta = jnp.sum(
                g_t.astype(jnp.float32) * att_t[b, :, cols].astype(jnp.float32),
                axis=0,
                keepdims=True,
            )
            held.append(
                (flipped_heads(q), stacked_heads(q), g_t, stacked_heads(g), delta, total_ref[b, :, cols])
            )

        def tile(step, mask, carry):
            low = low_of(step, odd, diag)
            k = keys[pl.ds(low, 256), :]
            k_t = k.T
            v = values[pl.ds(low, 256), :]
            result = []
            key_part = value_part = None
            for at, (q_t, q_s, g_t, g_s, delta, log_total) in enumerate(held):
                s = dot(k, q_t) * SCALE_LOG2
                if mask is not None:
                    s = jnp.where(mask, s, MASKED)
                p = jnp.exp2(s - log_total).astype(jnp.bfloat16)
                dp = dot(v, g_t)
                ds = (p.astype(jnp.float32) * (dp - delta)).astype(jnp.bfloat16)
                value_term, key_term, query_term = dot(p, g_s), dot(ds, q_s), dot(k_t, ds)
                value_part = value_term if value_part is None else value_part + value_term
                key_part = key_term if key_part is None else key_part + key_term
                result.append(query_term if carry is None else carry[at] + query_term)
            value_acc[pl.ds(low, 256), :] += value_part
            key_acc[pl.ds(low, 256), :] += key_part
            return result

        carry = tile(0, first_mask(odd, BW), None)
        carry = lax.fori_loop(1, steps, lambda step, carry: tile(step, None, carry), carry)
        for cols, dq_t in zip(groups, carry):
            dq_t = (dq_t * SCALE).astype(jnp.bfloat16)
            for head in range(BW // HD):
                at = cols.start + head * HD
                dq[block_rows(b), at : at + HD] = dq_t[:, head * HD : (head + 1) * HD].T
        outward(b).start()
        return _

    lax.fori_loop(0, BLK_DEV, block, 0)

    if last:
        near_at = ROWS - BLOCK
        own_at = PRIOR * BLOCK
        for acc, earlier, cols, factor in (
            (key_acc, key_in, slice(0, HD), SCALE),
            (value_acc, value_in, slice(HD, 2 * HD), 1.0),
        ):
            def total(rows):
                return (acc[rows] + earlier[rows]) * factor

            far_ref[:, cols] = total(slice(0, near_at)).astype(jnp.bfloat16)
            near_ref[:, cols] = total(slice(near_at, own_at)).astype(jnp.bfloat16)
            own_ref[:, cols] = total(slice(own_at, None))
    for b in range(BLK_DEV):
        outward(b).wait()


def backward(table, queries, att_t, totals, pool, sources, carried, chunk, last):
    first = carried is None
    pool_shape = (POOL * BLOCK, HD)
    sums = [jax.ShapeDtypeStruct(pool_shape, jnp.float32)] * 2
    if last:
        out_shape = [
            jax.ShapeDtypeStruct((ROWS, 2 * HD), jnp.float32),
            jax.ShapeDtypeStruct((ROWS, 2 * HD), jnp.bfloat16),
            jax.ShapeDtypeStruct((FAR_ROWS, 2 * HD), jnp.bfloat16),
        ]
        scratch = [pltpu.VMEM(pool_shape, jnp.float32)] * 2
    else:
        out_shape, scratch = sums, []

    def kernel(*refs):
        backward_kernel(chunk, last, first, *refs)

    return pl.pallas_call(
        kernel,
        in_specs=[SMEM] + [WHOLE] * 5 + [ANY] * 4 + ([] if first else [ANY, WHOLE, WHOLE]),
        out_specs=[ANY] + [WHOLE] * len(out_shape),
        out_shape=[jax.ShapeDtypeStruct((ROWS, WIDTH), jnp.bfloat16)] + out_shape,
        input_output_aliases={} if first else {10: 0},
        scratch_shapes=scratch
        + [
            pltpu.VMEM((ROWS, CW), jnp.bfloat16),
            pltpu.VMEM((ROWS, CW), jnp.bfloat16),
            pltpu.SemaphoreType.DMA((BLK_DEV,)),
            pltpu.SemaphoreType.DMA((BLK_DEV,)),
        ],
        compiler_params=PARAMS,
        cost_estimate=lasting(9),
        name="attention_backward",
    )(table, queries, att_t, totals, *pool, *sources, *([] if first else carried))


def grad_matmul_kernel(table, *refs):
    pieces, weight_hbm, outs = refs[:8], refs[8], refs[9 : 9 + CHUNKS]
    weight, sems = refs[9 + CHUNKS :]
    half = ROWS // 2
    copies = []
    for chunk in range(CHUNKS):
        for ahead in range(4):
            at = pl.multiple_of(((table[TP] + ahead) % 4) * WIDTH, WIDTH)
            copies.append(
                pltpu.make_async_copy(
                    weight_hbm.at[pl.ds(chunk * CW, CW), pl.ds(at, WIDTH)],
                    weight.at[4 * chunk + ahead],
                    sems.at[4 * chunk + ahead],
                )
            )
            copies[-1].start()
    for chunk in range(CHUNKS):
        totals = [None, None]
        for ahead in range(4):
            slot = 4 * chunk + ahead
            copies[slot].wait()
            for part in range(2):
                term = dot_nt(pieces[2 * ahead + part][...], weight[slot])
                totals[part] = term if totals[part] is None else totals[part] + term
        for part in range(2):
            outs[chunk][part * half : (part + 1) * half] = totals[part].astype(jnp.bfloat16)


def grad_matmul(table, pieces, weight):
    return pl.pallas_call(
        grad_matmul_kernel,
        in_specs=[SMEM] + [WHOLE] * 8 + [ANY],
        out_specs=[WHOLE] * CHUNKS,
        out_shape=[jax.ShapeDtypeStruct((ROWS, CW), jnp.bfloat16)] * CHUNKS,
        scratch_shapes=[
            pltpu.VMEM((4 * CHUNKS, CW, WIDTH), jnp.bfloat16),
            pltpu.SemaphoreType.DMA((4 * CHUNKS,)),
        ],
        compiler_params=PARAMS,
        cost_estimate=lasting(7),
        name="grad_projection",
    )(table, *pieces, weight)


HALF = WIDTH // 2


def weight_copy(table, weight_hbm, weight, slot, ahead, half, sem):
    at = pl.multiple_of(((table[TP] + ahead) % 4) * WIDTH + half * HALF, HALF)
    return pltpu.make_async_copy(weight_hbm.at[:, pl.ds(at, HALF)], weight.at[slot], sem)


def product_kernel(table, *refs):
    sources = [refs[4 * c : 4 * c + 4] for c in range(CHUNKS)]
    weight_hbm, left, right, onward, back, own, rows, weight, sems, weight_sems = refs[4 * CHUNKS :]

    def place(c, at):
        return rows.at[block_rows(at), pl.ds(c * CW, CW)]

    places = [(c, at, c * BLK_DEV + at) for c in range(CHUNKS) for at in range(BLK_DEV)]
    for c, at, sem in places:
        start_chosen(
            table[ATT_REL + at], table[ATT_IDX + at], sources[c], place(c, at), sems.at[sem]
        )
    parts = ((2, 0), (2, 1), (1, 1), (3, 0), (0, 0), (0, 1))
    weights = [
        weight_copy(table, weight_hbm, weight, slot, ahead, half, weight_sems.at[slot])
        for slot, (ahead, half) in enumerate(parts)
    ]
    for copy in weights:
        copy.start()
    for c, at, sem in places:
        pltpu.make_async_copy(sources[c][0].at[pl.ds(0, BLOCK)], place(c, at), sems.at[sem]).wait()
    for slot, out in enumerate((left, right, onward, back)):
        weights[slot].wait()
        out[...] = dot(rows[...], weight[slot]).astype(jnp.bfloat16)
    for slot in (4, 5):
        weights[slot].wait()
        own[:, (slot - 4) * HALF : (slot - 3) * HALF] = dot(rows[...], weight[slot]).astype(
            jnp.bfloat16
        )


def products(table, sources, weight):
    flat = [source for group in sources for source in group]
    return pl.pallas_call(
        product_kernel,
        in_specs=[SMEM] + [ANY] * (4 * CHUNKS + 1),
        out_specs=[WHOLE] * 6,
        out_shape=[jax.ShapeDtypeStruct((ROWS, HALF), jnp.bfloat16)] * 4
        + [jax.ShapeDtypeStruct((ROWS, WIDTH), jnp.bfloat16)] * 2,
        scratch_shapes=[
            pltpu.VMEM((6, WIDTH, HALF), jnp.bfloat16),
            pltpu.SemaphoreType.DMA((4 * CHUNKS,)),
            pltpu.SemaphoreType.DMA((6,)),
        ],
        compiler_params=PARAMS,
        cost_estimate=lasting(7),
        name="products",
    )(table, *flat, weight)


def sum_product_kernel(table, rows, weight_hbm, before, after_, onward, back, weight, sems):
    weights = [
        weight_copy(table, weight_hbm, weight, 0, 1, 0, sems.at[0]),
        weight_copy(table, weight_hbm, weight, 1, 3, 1, sems.at[1]),
    ]
    for copy in weights:
        copy.start()
    for slot, (extra, out) in enumerate(((before, onward), (after_, back))):
        weights[slot].wait()
        value = dot(rows[...], weight[slot])
        out[...] = (value + extra[...].astype(jnp.float32)).astype(jnp.bfloat16)


def sum_products(table, rows, weight, before, after):
    half = jax.ShapeDtypeStruct((ROWS, HALF), jnp.bfloat16)
    return pl.pallas_call(
        sum_product_kernel,
        in_specs=[SMEM, WHOLE, ANY, WHOLE, WHOLE],
        out_specs=[WHOLE] * 2,
        out_shape=[half] * 2,
        scratch_shapes=[
            pltpu.VMEM((2, WIDTH, HALF), jnp.bfloat16),
            pltpu.SemaphoreType.DMA((2,)),
        ],
        compiler_params=PARAMS,
        cost_estimate=lasting(4),
        name="sum_products",
    )(table, rows, weight, before, after)


def last_sum_kernel(own, before_a, before_b, after_a, after_b, out):
    for half, before, after in ((0, before_a, after_a), (1, before_b, after_b)):
        cols = slice(half * 512, (half + 1) * 512)
        out[:, cols] = (
            own[:, cols].astype(jnp.float32) + before[...].astype(jnp.float32) + after[...].astype(jnp.float32)
        ).astype(jnp.bfloat16)


def last_sum(own, before_a, before_b, after_a, after_b):
    part = pl.BlockSpec((BLOCK, 512), lambda j: (j, 0))
    full = pl.BlockSpec((BLOCK, WIDTH), lambda j: (j, 0))
    return pl.pallas_call(
        last_sum_kernel,
        grid=(4,),
        in_specs=[full, part, part, part, part],
        out_specs=full,
        out_shape=jax.ShapeDtypeStruct((ROWS, WIDTH), jnp.bfloat16),
        compiler_params=PARAMS,
        cost_estimate=lasting(2),
        name="last_sum",
    )(own, before_a, before_b, after_a, after_b)


def scalar_table(doc_start, balanced_source):
    device = lax.axis_index("cp")
    member = device % GROUP
    group_blocks = GROUP * BLK_DEV
    group_first = device // GROUP * group_blocks
    sources = lax.dynamic_slice_in_dim(balanced_source, group_first, group_blocks) - group_first
    slots = jnp.arange(group_blocks, dtype=jnp.int32)
    slot_of = jnp.sum(
        jnp.where(sources[None, :] == slots[:, None], slots[None, :], 0), axis=1, dtype=jnp.int32
    )
    mine = member * BLK_DEV
    wanted = lax.dynamic_slice_in_dim(sources, mine, BLK_DEV)
    held = lax.dynamic_slice_in_dim(slot_of, mine, BLK_DEV)
    starts = lax.dynamic_slice_in_dim(doc_start, device * BLK_DEV, BLK_DEV)
    starts = starts - (device * BLK_DEV - PRIOR)
    return jnp.concatenate(
        [
            starts,
            (held // BLK_DEV) ^ member,
            held % BLK_DEV,
            (wanted // BLK_DEV) ^ member,
            wanted % BLK_DEV,
            jnp.stack([device % 2, lax.axis_index("tp")]),
        ]
    ).astype(jnp.int32)


def group_exchange(block, earlier):
    across = swap_cp(block, 2)
    return [block, swap_cp(after(block, earlier), 1), across, swap_cp(after(across, earlier), 1)]


def copy_all(*pairs, sems):
    copies = [pltpu.make_async_copy(src, dst, sems.at[at]) for at, (src, dst) in enumerate(pairs)]
    for copy in copies:
        copy.start()
    for copy in copies:
        copy.wait()


def join_kernel(keys, values, grads, kv, last, upper, lower, sems):
    half = ROWS // 2
    tail = pl.ds(ROWS - FAR_ROWS, FAR_ROWS)
    left, right = pl.ds(0, HD), pl.ds(HD, HD)
    copy_all(
        (keys, kv.at[:, left]),
        (values, kv.at[:, right]),
        (keys.at[tail], last.at[:, left]),
        (values.at[tail], last.at[:, right]),
        (grads.at[pl.ds(0, half)], upper),
        (grads.at[pl.ds(half, half)], lower),
        sems=sems,
    )


def join(keys, values, grads):
    return pl.pallas_call(
        join_kernel,
        in_specs=[HBM] * 3,
        out_specs=[WHOLE] * 4,
        out_shape=[
            jax.ShapeDtypeStruct((ROWS, 2 * HD), jnp.bfloat16),
            jax.ShapeDtypeStruct((FAR_ROWS, 2 * HD), jnp.bfloat16),
        ]
        + [jax.ShapeDtypeStruct((ROWS // 2, WIDTH), jnp.bfloat16)] * 2,
        scratch_shapes=[pltpu.SemaphoreType.DMA((6,))],
        compiler_params=PARAMS,
        cost_estimate=lasting(2),
        name="join",
    )(keys, values, grads)


def add_kernel(own, near, far, keys, values):
    total = own[...] + near[...].astype(jnp.float32)
    front = total[: ROWS - FAR_ROWS].astype(jnp.bfloat16)
    rear = (total[ROWS - FAR_ROWS :] + far[...].astype(jnp.float32)).astype(jnp.bfloat16)
    for col, out in ((0, keys), (HD, values)):
        out[: ROWS - FAR_ROWS] = front[:, col : col + HD]
        out[ROWS - FAR_ROWS :] = rear[:, col : col + HD]


def add_terms(own, near, far):
    return pl.pallas_call(
        add_kernel,
        in_specs=[WHOLE] * 3,
        out_specs=[WHOLE] * 2,
        out_shape=[jax.ShapeDtypeStruct((ROWS, HD), jnp.bfloat16)] * 2,
        compiler_params=PARAMS,
        cost_estimate=lasting(1),
        name="add_terms",
    )(own, near, far)


def after(value, earlier):
    return lax.optimization_barrier((value, earlier))[0]


def shards(queries, key_rows, value_rows, out_proj, grad_mixed, doc_start, balanced_source):
    table = scalar_table(doc_start, balanced_source)

    kv, last, upper, lower = join(key_rows, value_rows, grad_mixed)
    far = shift_cp(last, 2)
    near = shift_cp(kv, 1)
    pool = (kv, far, near)

    before_upper = shift_tp(upper, 1)
    ahead_lower = shift_tp(lower, -1)
    before_lower = shift_tp(lower, 1)
    ahead_upper = shift_tp(upper, -1)

    attended, attended_t, totals = [], [], []
    for chunk in range(CHUNKS):
        att, att_t, total, *laid_out = forward(
            after(table, (attended[0], before_upper, ahead_lower))
            if chunk
            else table,
            queries,
            pool,
            chunk,
        )
        if chunk == 0:
            pool = laid_out
            opposite = [
                shift_tp(after(before_upper, att), 1),
                shift_tp(after(ahead_lower, att), -1),
            ]
        attended.append(att)
        attended_t.append(att_t)
        totals.append(total)

    pieces = (upper, lower, ahead_upper, ahead_lower, *opposite, before_upper, before_lower)
    exchanged = [group_exchange(attended[0], attended[1]), None]
    grad_attended = grad_matmul(table, pieces, out_proj)
    across = swap_cp(after(attended[1], (before_lower, ahead_upper)), 2)
    exchanged[1] = [
        attended[1],
        swap_cp(after(attended[1], grad_attended[1]), 1),
        across,
        swap_cp(after(across, grad_attended[1]), 1),
    ]
    grad_across = swap_cp(grad_attended[0], 2)

    far_left, far_right, onward_b, back_a, own, rows = products(
        after(table, grad_attended[1]), exchanged, out_proj
    )
    from_before = shift_tp(far_left, 1)
    from_after = shift_tp(far_right, -1)

    grad_sources = [
        [
            grad_attended[0],
            swap_cp(after(grad_attended[0], own), 1),
            grad_across,
            swap_cp(after(grad_across, own), 1),
        ]
    ]
    swapped = swap_cp(grad_attended[1], 1)
    carried = backward(
        after(table, (own, swapped)),
        queries, attended_t[0], totals[0], pool, grad_sources[0], None, 0, False,
    )
    query_a = carried[1]
    across = swap_cp(after(grad_attended[1], grad_across), 2)
    grad_sources.append(
        [
            grad_attended[1],
            swapped,
            across,
            swap_cp(after(across, query_a), 1),
        ]
    )
    before_b = shift_tp(onward_b, 1)
    after_a = shift_tp(back_a, -1)
    onward_a, back_b = sum_products(
        after(table, query_a), rows, out_proj, from_before, from_after)
    before_a = shift_tp(onward_a, 1)
    after_b = shift_tp(back_b, -1)
    query_grad, own_grads, near_grads, far_grads = backward(
        after(table, onward_a),
        queries, attended_t[1], totals[1], pool, grad_sources[1], carried, 1, True,
    )
    far_back = shift_cp(after(far_grads, (before_b, after_a)), -2)
    near_back = shift_cp(after(near_grads, (before_b, after_a)), -1)
    mixed = last_sum(own, before_a, before_b, after_a, after_b)
    key_grad, value_grad = add_terms(after(own_grads, mixed), near_back, far_back)
    return (mixed, query_grad, key_grad, value_grad)


def solution(mesh):
    placed = (P("cp", "tp"), P("cp", "tp"), P("cp", "tp"), P("tp", None), P("cp", "tp"), P(), P())
    return jax.shard_map(
        shards,
        mesh=mesh,
        in_specs=placed,
        out_specs=(P("cp", "tp"),) * 4,
        check_vma=False,
    )
```
